512 devices in a mesh: rep: 32 (over y_lo, z, core), fsdp: 16 (over y_hi, x).
Axes of the slice: x: 4, y: 8 (y_hi: 4, y_lo: 2; y = y_hi * 2 + y_lo), z: 8, core: 2. Of those that a mesh axis runs over, the one named last changes fastest.
Arguments:
- attn_out: bfloat16 [81920, 2560], P('rep', 'fsdp'), may hold values from -6 to 6
- out_grad: bfloat16 [81920, 2560], P(('rep', 'fsdp')), may hold values from -6 to 6
- momentum: bfloat16 [32, 2560, 2560], P('rep', 'fsdp'), may hold values from -6 to 6
- kept: int32 [16], replicated, may hold values from 0 to 63, as said below
Outputs:
- update: bfloat16 [2560, 2560], P('fsdp')
- new_momentum: bfloat16 [32, 2560, 2560], P('rep', 'fsdp')
The draws below stay inside these ranges and needn't reach their ends.
Inputs may be any that keep to these rules, and one draw needn't show every extreme that they name: `kept`: 16 distinct frequencies, among them 0 and 63.
All inputs are finite; a program needn't handle non-finite values.
Results may differ from the reference program's by a relative error of at most 0.001.
Values may be sent and summed in bfloat16 or wider, within the bound.
No kernel may reach another device: no remote copies, remote signals or barrier semaphores. Data moves between devices by JAX's collectives and lax.ppermute only.
A program may use at most 64 MiB of HBM per device.

```python
import math
import jax
import jax.numpy as jnp
from jax import lax

HEADS = 20
HEAD_DIM = 128
WIDTH = 2560
GROUP = 64
KEEP = 16
TOK_DEV = 160
IN_W = 2560
TOKENS = 81920
REPLICAS = 32
N_REP = 32
N_FSDP = 16


def draw_kept(key, part):
    key = jax.random.fold_in(key, 7)
    middle = jax.random.permutation(key, GROUP - 2)[:KEEP - 2].astype(jnp.int32) + 1
    return jnp.concatenate([jnp.zeros((1,), jnp.int32), middle, jnp.full((1,), GROUP - 1, jnp.int32)])


def shard_levels(key, shape, split, smallest, top_value):
    def one(axis_at, parts):
        steps = jax.random.uniform(jax.random.fold_in(jax.random.fold_in(key, 6), axis_at), (parts,), jnp.float32, smallest / len(split), top_value / len(split))
        return jnp.repeat(jnp.exp(steps), shape[axis_at] // parts).reshape((-1,) + (1,) * (len(shape) - axis_at - 1))

    gain = one(*split[0])
    for cut in split[1:]:
        gain = gain * one(*cut)
    return gain


def noise(key, shape, scale, bound, shards=(), kind=jnp.bfloat16):
    values = jax.random.normal(key, shape, jnp.float32) * scale
    if len(shards) > 0:
        values = shard_levels(key, shape, shards, -0.22, 0.18) * values
    return jnp.clip(values, min=-bound, max=bound).astype(kind)


def setup_inputs(seed: int = 0) -> dict:
    key_list = jax.random.split(jax.random.key(seed), 5)
    attn_out = noise(key_list[0], (TOKENS, IN_W), 1.0, 6.0, ((0, 32), (1, 16)))
    out_grad = noise(key_list[1], (TOKENS, WIDTH), 1.0, 6.0, ((0, 512),))
    momentum = noise(key_list[2], (REPLICAS, IN_W, WIDTH), 1.0, 6.0, ((0, 32), (1, 16)))
    kept = draw_kept(jax.random.fold_in(key_list[4], 71), 0)
    return {"attn_out": attn_out, "out_grad": out_grad, "momentum": momentum, "kept": kept}


BETA = 0.999

def basis_table(kept):
    freq = kept.astype(jnp.float32)
    points = jnp.arange(GROUP, dtype=jnp.float32) + 0.5
    weight = jnp.where(kept == 0, math.sqrt(1.0 / GROUP), math.sqrt(2.0 / GROUP)).astype(jnp.float32)
    return weight[None, :] * jnp.cos(math.pi * points[:, None] * freq[None, :] / GROUP)

def encode(moment, basis):
    rows, width = moment.shape
    blocks = moment.reshape(rows, width // GROUP, GROUP)
    coeff = jnp.einsum('rcn,nk->rck', blocks, basis, precision=lax.Precision.HIGHEST)
    return coeff.reshape(rows, width // GROUP * KEEP)

def decode(coeff, basis):
    rows = coeff.shape[0]
    blocks = coeff.reshape(rows, coeff.shape[1] // KEEP, KEEP)
    values = jnp.einsum('rck,nk->rcn', blocks, basis, precision=lax.Precision.HIGHEST)
    return values.reshape(rows, values.shape[1] * GROUP)

def reference(attn_out, out_grad, momentum, kept):
    basis = basis_table(kept)
    tok_rep = TOK_DEV * N_FSDP
    scale = 1.0 / math.sqrt(tok_rep)

    def one_replica(carry, index):
        acts = lax.dynamic_slice_in_dim(attn_out, index * tok_rep, tok_rep, 0)
        cotan = lax.dynamic_slice_in_dim(out_grad, index * tok_rep, tok_rep, 0)
        grad = lax.dot_general(acts, cotan, (((0,), (0,)), ((), ())), preferred_element_type=jnp.float32) * scale
        moment = BETA * momentum[index].astype(jnp.float32) + grad
        coeff = encode(moment, basis)
        fresh = (moment - decode(coeff, basis)).astype(jnp.bfloat16)
        return (carry + coeff, fresh)
    start = jnp.zeros((HEADS * HEAD_DIM, WIDTH // GROUP * KEEP), jnp.float32)
    total, new_momentum = lax.scan(one_replica, start, jnp.arange(N_REP, dtype=jnp.int32))
    update = decode(total / N_REP, basis).astype(jnp.bfloat16)
    return (update, new_momentum)
```

```python
import math

import jax
import jax.numpy as jnp
from jax import lax
from jax.experimental import pallas as pl
from jax.experimental.pallas import tpu as pltpu
from jax.sharding import Mesh, PartitionSpec as P

GROUP = 64
KEEP = 16
BETA = 0.999

REP = ("ylo", "z", "core")
FSDP = ("yhi", "x")


def basis_table(kept):
    freq = kept.astype(jnp.float32)
    points = jnp.arange(GROUP, dtype=jnp.float32) + 0.5
    weight = jnp.where(kept == 0, math.sqrt(1.0 / GROUP), math.sqrt(2.0 / GROUP)).astype(
        jnp.float32
    )
    return weight[None, :] * jnp.cos(math.pi * points[:, None] * freq[None, :] / GROUP)


def block_basis(basis, groups):
    tiled = jnp.tile(basis, (groups, groups))
    row = lax.broadcasted_iota(jnp.int32, tiled.shape, 0) // GROUP
    col = lax.broadcasted_iota(jnp.int32, tiled.shape, 1) // KEEP
    return jnp.where(row == col, tiled, 0.0)


def dot_f32(a, b, dims):
    return lax.dot_general(
        a, b, (dims, ((), ())), precision=lax.Precision.HIGHEST, preferred_element_type=jnp.float32
    )


def product_kernel(
    scale, where_ref, acts_ref, own_ref, pa_ref, pb_ref, ma_ref, mb_ref, fa_ref, fb_ref,
    mom_ref, basis_ref, fresh_ref, keep_ref, send_ref,
):
    yhi = where_ref[0]
    core = where_ref[1]
    depth = own_ref.shape[0]
    half = depth // 2

    def acts(shift, start, size):
        at = lax.rem(yhi + shift, 4) * depth
        block = acts_ref[:, pl.ds(pl.multiple_of(at, depth), depth)]
        return block[:, start : start + size]

    def mul(a, b_ref):
        return jnp.dot(a, b_ref[...], preferred_element_type=jnp.float32)

    grad = mul(acts(0, 0, depth), own_ref)
    grad += jnp.dot(
        acts(3, 0, depth), jnp.concatenate([pa_ref[...], pb_ref[...]], 0),
        preferred_element_type=jnp.float32,
    )
    grad += jnp.dot(
        acts(1, 0, depth), jnp.concatenate([ma_ref[...], mb_ref[...]], 0),
        preferred_element_type=jnp.float32,
    )
    grad += jnp.dot(
        acts(2, 0, depth), jnp.concatenate([fa_ref[...], fb_ref[...]], 0),
        preferred_element_type=jnp.float32,
    )
    moment = BETA * mom_ref[...].astype(jnp.float32) + grad * scale
    basis = basis_ref[...]
    coeff = dot_f32(moment, basis, ((1,), (0,)))
    fresh_ref[...] = (moment - dot_f32(coeff, basis, ((1,), (1,)))).astype(jnp.bfloat16)
    rows = coeff.shape[0] // 2
    low, high = coeff[:rows], coeff[rows:]
    keep_ref[0] = jnp.where(core == 0, low, high)
    send_ref[0] = jnp.where(core == 0, high, low)


def product(scale, where, acts, own, parts, mom, basis):
    feats, toks = acts.shape
    outs = own.shape[1]
    nrow = feats // 4
    coefs = basis.shape[1]
    whole = lambda a: pl.BlockSpec(a.shape, lambda p: (0,) * a.ndim)
    half = jax.ShapeDtypeStruct((4, nrow // 2, coefs), jnp.float32)
    return pl.pallas_call(
        lambda *refs: product_kernel(scale, *refs),
        grid=(4,),
        in_specs=[
            pl.BlockSpec(memory_space=pltpu.SMEM),
            pl.BlockSpec((nrow, toks), lambda p: (p, 0)),
            whole(own),
            *[whole(a) for a in parts],
            pl.BlockSpec((nrow, outs), lambda p: (p, 0)),
            whole(basis),
        ],
        out_specs=[
            pl.BlockSpec((nrow, outs), lambda p: (p, 0)),
            pl.BlockSpec((1, nrow // 2, coefs), lambda p: (p, 0, 0)),
            pl.BlockSpec((1, nrow // 2, coefs), lambda p: (p, 0, 0)),
        ],
        out_shape=[jax.ShapeDtypeStruct((feats, outs), jnp.bfloat16), half, half],
        compiler_params=pltpu.CompilerParams(vmem_limit_bytes=32 * 1024 * 1024),
        cost_estimate=pl.CostEstimate(
            flops=2 * feats * toks * outs + 24 * feats * outs * coefs,
            bytes_accessed=2 * (feats * toks + toks * outs + 2 * feats * outs) + 8 * feats * coefs,
            transcendentals=0,
        ),
    )(where, acts, own, *parts, mom, basis)


def decode_kernel(replicas, total_ref, basis_ref, out_ref):
    mean = total_ref[0] / replicas
    out_ref[...] = dot_f32(mean, basis_ref[...], ((1,), (1,))).astype(jnp.bfloat16)


def decode(replicas, total, basis):
    quarters, rows, coefs = total.shape
    outs = basis.shape[0]
    return pl.pallas_call(
        lambda *refs: decode_kernel(replicas, *refs),
        grid=(quarters,),
        in_specs=[
            pl.BlockSpec((1, rows, coefs), lambda q: (q, 0, 0)),
            pl.BlockSpec(basis.shape, lambda q: (0, 0)),
        ],
        out_specs=pl.BlockSpec((rows, outs), lambda q: (0, q)),
        out_shape=jax.ShapeDtypeStruct((rows, quarters * outs), jnp.bfloat16),
        cost_estimate=pl.CostEstimate(
            flops=12 * quarters * rows * coefs * outs,
            bytes_accessed=4 * quarters * rows * coefs + 2 * quarters * rows * outs,
            transcendentals=0,
        ),
    )(total, basis)


def shifted(x, axis, size, by):
    return lax.ppermute(x, axis, [(i, (i + by) % size) for i in range(size)])


def per_device(attn_out, out_grad, momentum, kept):
    replicas = 32
    scale = 1.0 / math.sqrt(attn_out.shape[0])
    toks, width = out_grad.shape
    half = 2 * toks

    own = lax.all_to_all(out_grad, "x", 1, 0, tiled=True)
    acts = lax.all_gather(attn_out.T, "x", axis=0, tiled=True)
    low, high = own[:half], own[half:]
    from_below_low = shifted(low, "yhi", 4, 1)
    from_above_high = shifted(high, "yhi", 4, -1)
    from_below_high = shifted(high, "yhi", 4, 1)
    from_above_low = shifted(low, "yhi", 4, -1)
    far_low = shifted(from_below_low, "yhi", 4, 1)
    far_high = shifted(from_above_high, "yhi", 4, -1)
    mom = lax.all_to_all(momentum[0], "x", 1, 0, tiled=True)

    basis = block_basis(basis_table(kept), width // 4 // GROUP)
    where = jnp.stack([lax.axis_index("yhi"), lax.axis_index("core")]).astype(jnp.int32)
    parts = (from_below_low, from_below_high, from_above_low, from_above_high, far_low, far_high)
    fresh, keep, send = product(scale, where, acts, own, parts, mom, basis)
    new_momentum = lax.all_to_all(fresh, "x", 0, 1, tiled=True)

    coefs = keep.shape[-1]
    pair = keep + shifted(send, "core", 2, 1)
    pieces = lax.all_to_all(pair.reshape(8, 40, coefs), ("x", "ylo"), 0, 0, tiled=True)
    summed = pieces.reshape(4, 2, 40, coefs).sum(1)
    pieces = lax.all_to_all(summed.reshape(8, 20, coefs), "z", 0, 0, tiled=True)
    summed = pieces.sum(0)
    spread = jnp.broadcast_to(summed[None], (16, 20, coefs))
    spread = lax.all_to_all(spread, ("ylo", "z"), 0, 0, tiled=True)
    spread = lax.all_gather(spread, "core", axis=0)
    total = spread.reshape(2, 2, 4, 2, 20, coefs).transpose(2, 0, 1, 3, 4, 5)
    update = decode(replicas, total.reshape(4, toks, coefs), basis)
    return update, new_momentum[None]


def solution(mesh):
    fine = Mesh(mesh.devices.reshape(2, 8, 2, 4, 4), ("ylo", "z", "core", "yhi", "x"))
    return jax.shard_map(
        per_device,
        mesh=fine,
        in_specs=(P(REP, FSDP), P(REP + FSDP, None), P(REP, FSDP, None), P()),
        out_specs=(P(FSDP, None), P(REP, FSDP, None)),
        check_vma=False,
    )
```

```python
import math

import jax
import jax.numpy as jnp
from jax import lax
from jax.experimental import pallas as pl
from jax.experimental.pallas import tpu as pltpu
from jax.sharding import Mesh, PartitionSpec as P

GROUP = 64
KEEP = 16
BETA = 0.999
SIDE = 4
STEPS = 2
LANES = 128

REP = ("ylo", "z", "core")
FSDP = ("yhi", "x")

SMEM = pl.BlockSpec(memory_space=pltpu.SMEM)
VMEM = pl.BlockSpec(memory_space=pltpu.VMEM)
HBM = pl.BlockSpec(memory_space=pltpu.HBM)


def room(mebibytes):
    return pltpu.CompilerParams(vmem_limit_bytes=mebibytes * 1024 * 1024)


def basis_table(kept):
    freq = kept.astype(jnp.float32)
    points = jnp.arange(GROUP, dtype=jnp.float32) + 0.5
    weight = jnp.where(kept == 0, math.sqrt(1.0 / GROUP), math.sqrt(2.0 / GROUP)).astype(
        jnp.float32
    )
    return weight[None, :] * jnp.cos(math.pi * points[:, None] * freq[None, :] / GROUP)


def cost(flops, *arrays):
    return pl.CostEstimate(
        flops=flops, bytes_accessed=sum(a.size * a.dtype.itemsize for a in arrays), transcendentals=0
    )


def two_parts(x):
    high = x.astype(jnp.bfloat16)
    return high, (x - high.astype(jnp.float32)).astype(jnp.bfloat16)


def dot_parts(a, b, dims):
    def one(x, y):
        return lax.dot_general(x, y, (dims, ((), ())), preferred_element_type=jnp.float32)

    return one(a[0], b[0]) + (one(a[0], b[1]) + one(a[1], b[0]))


def quarter_kernel(where_ref, grad_ref, out_ref):
    width = out_ref.shape[1]
    at = where_ref[0] * width
    out_ref[...] = grad_ref[:, pl.ds(pl.multiple_of(at, width), width)]


def quarter(where, whole):
    rows, width = whole.shape
    out = jax.ShapeDtypeStruct((rows, width // SIDE), whole.dtype)
    return pl.pallas_call(
        quarter_kernel,
        in_specs=[SMEM, VMEM],
        out_specs=VMEM,
        out_shape=out,
        compiler_params=room(4),
        cost_estimate=cost(0, out, out),
    )(where, whole)


def pack_kernel(whole_ref, out_ref):
    width = out_ref.shape[2]
    for q in range(SIDE):
        out_ref[q] = whole_ref[:, q * width : (q + 1) * width]


def pack(whole, weight=1):
    rows, width = whole.shape
    out = jax.ShapeDtypeStruct((SIDE, rows, width // SIDE), whole.dtype)
    return pl.pallas_call(
        pack_kernel,
        in_specs=[VMEM],
        out_specs=VMEM,
        out_shape=out,
        compiler_params=room(4),
        cost_estimate=cost(0, *[out] * weight),
    )(whole)


def others_kernel(where_ref, all_ref, out_ref):
    rows = all_ref.shape[1]
    for n in range(SIDE - 1):
        out_ref[n * rows : (n + 1) * rows] = all_ref[lax.rem(where_ref[0] + n + 1, SIDE)]


def others(where, every):
    _, toks, width = every.shape
    return pl.pallas_call(
        others_kernel,
        in_specs=[SMEM, VMEM],
        out_specs=VMEM,
        out_shape=jax.ShapeDtypeStruct(((SIDE - 1) * toks, width), every.dtype),
        compiler_params=room(4),
        cost_estimate=cost(0, every, every),
    )(where, every)


def rows_in_order(where_ref, piece_refs, block, sems):
    each = block.shape[0] // SIDE
    copies = []
    row = 0
    for piece_ref in piece_refs:
        start = row
        while row < start + piece_ref.shape[0]:
            n, skip = divmod(row, each)
            size = min(each - skip, start + piece_ref.shape[0] - row)
            at = pl.multiple_of(lax.rem(where_ref[0] + n, SIDE) * each + skip, each // 2)
            copies.append(
                pltpu.make_async_copy(
                    piece_ref.at[pl.ds(row - start, size)], block.at[pl.ds(at, size)], sems.at[len(copies)]
                )
            )
            row += size
    return copies


def acts_columns(where_ref, shift, acts_ref, depth):
    at = lax.rem(where_ref[1] + shift, SIDE) * depth
    return acts_ref.at[:, pl.ds(pl.multiple_of(at, depth), depth)]


def near_kernel(scale, where_ref, acts_ref, mom_ref, table_ref, *rest):
    pieces, rest = rest[:6], rest[6:]
    part_ref, coeff_ref, high_ref, low_ref, grad_block, sems = rest
    depth = grad_block.shape[0] // 3

    @pl.when(pl.program_id(0) == 0)
    def _():
        copies = []
        for n in range(3):
            block = grad_block.at[n * depth : (n + 1) * depth]
            copies += rows_in_order(where_ref, pieces[2 * n : 2 * n + 2], block, sems.at[n])
        for copy in copies:
            copy.start()
        rows, coefs = high_ref.shape
        table = jnp.concatenate([table_ref[...]] * (rows // GROUP), 0)
        row = lax.broadcasted_iota(jnp.int32, (rows, coefs), 0) // GROUP
        col = lax.broadcasted_iota(jnp.int32, (rows, coefs), 1) // KEEP
        high_ref[...], low_ref[...] = two_parts(jnp.where(row == col, table, 0.0))
        for copy in copies:
            copy.wait()

    total = None
    for n, shift in enumerate((0, 3, 1)):
        at = pl.multiple_of(lax.rem(where_ref[1] + shift, SIDE) * depth, depth)
        term = jnp.dot(
            acts_ref[:, pl.ds(at, depth)], grad_block[n * depth : (n + 1) * depth],
            preferred_element_type=jnp.float32,
        )
        total = term if total is None else total + term
    part = BETA * mom_ref[...].astype(jnp.float32) + total * scale
    part_ref[...] = part
    coeff_ref[...] = dot_parts(two_parts(part), (high_ref[...], low_ref[...]), ((1,), (0,)))


def near(scale, where, acts, mom, table, pieces, weight=1):
    feats, toks = acts.shape
    rows = feats // STEPS
    outs = pieces[0].shape[1]
    coefs = table.shape[1]
    part = jax.ShapeDtypeStruct((feats, outs), jnp.float32)
    coeff = jax.ShapeDtypeStruct((feats, coefs), jnp.float32)
    basis = jax.ShapeDtypeStruct((outs, coefs), jnp.bfloat16)
    some = pl.BlockSpec((rows, outs), lambda p, w: (p, 0))
    whole = pl.BlockSpec(basis.shape, lambda p, w: (0, 0))
    return pl.pallas_call(
        lambda *refs: near_kernel(scale, *refs),
        grid_spec=pltpu.PrefetchScalarGridSpec(
            num_scalar_prefetch=1,
            grid=(STEPS,),
            in_specs=[
                pl.BlockSpec((rows, toks), lambda p, w: (p, 0)),
                some,
                pl.BlockSpec(table.shape, lambda p, w: (0, 0)),
                *[HBM] * len(pieces),
            ],
            out_specs=[some, pl.BlockSpec((rows, coefs), lambda p, w: (p, 0)), whole, whole],
            scratch_shapes=[
                pltpu.VMEM((3 * toks // SIDE, outs), jnp.bfloat16),
                pltpu.SemaphoreType.DMA((3, SIDE)),
            ],
        ),
        out_shape=[part, coeff, basis, basis],
        compiler_params=room(60),
        cost_estimate=cost(weight * 3 * feats * toks * outs // 2, acts, part, *pieces),
    )(where, acts, mom, table, *pieces)


def packed(coeff, rows):
    wide = coeff.shape[1] - LANES
    rest = [coeff[n : n + 8, LANES:] for n in range(0, coeff.shape[0], 8)]
    rest += [jnp.zeros_like(rest[0])] * (-len(rest) % (LANES // wide))
    tiles = [
        jnp.concatenate(rest[n : n + LANES // wide], 1) for n in range(0, len(rest), LANES // wide)
    ]
    blank = jnp.zeros((rows - coeff.shape[0] - 8 * len(tiles), LANES), coeff.dtype)
    return jnp.concatenate([coeff[:, :LANES], *tiles, blank], 0)


def unpacked(tiles, rows, coefs):
    wide = coefs - LANES
    rest = []
    for n in range(rows // 8):
        row, lane = rows + 8 * (n // (LANES // wide)), wide * (n % (LANES // wide))
        rest.append(tiles[row : row + 8, lane : lane + wide])
    return jnp.concatenate([tiles[:rows], jnp.concatenate(rest, 0)], 1)


def far_kernel(
    scale, where_ref, acts_ref, near_ref, high_ref, low_ref, p0_ref, p1_ref, p2_ref, p3_ref,
    coeff_ref, packed_ref, acts_block, grad_block, sems,
):
    depth = grad_block.shape[0]
    copies = rows_in_order(where_ref, (p0_ref, p1_ref, p2_ref, p3_ref), grad_block, sems)
    last = pltpu.make_async_copy(
        acts_columns(where_ref, 2, acts_ref, depth), acts_block, sems.at[6]
    )
    for copy in [*copies, last]:
        copy.start()
    for copy in copies:
        copy.wait()

    def dot(a, b):
        return jnp.dot(a, b, preferred_element_type=jnp.float32)

    grad = grad_block[...]
    high, low = two_parts(dot(grad, high_ref[...]) + dot(grad, low_ref[...]))
    last.wait()
    acts = acts_block[...]
    coeff = near_ref[...] + (dot(acts, high) + dot(acts, low)) * scale
    coeff_ref[...] = coeff
    count, rows, _ = packed_ref.shape
    each = coeff.shape[0] // count
    for n in range(count):
        packed_ref[n] = packed(coeff[n * each : (n + 1) * each], rows)


def far(scale, where, acts, coeff, high, low, pieces):
    outs, coefs = high.shape
    feats = acts.shape[0]
    depth = acts.shape[1] // SIDE
    out = jax.ShapeDtypeStruct((16, 64, LANES), jnp.float32)
    return pl.pallas_call(
        lambda *refs: far_kernel(scale, *refs),
        in_specs=[SMEM, HBM] + [VMEM] * 3 + [HBM] * len(pieces),
        out_specs=[VMEM] * 2,
        out_shape=[jax.ShapeDtypeStruct(coeff.shape, coeff.dtype), out],
        scratch_shapes=[
            pltpu.VMEM((feats, depth), jnp.bfloat16),
            pltpu.VMEM((depth, outs), jnp.bfloat16),
            pltpu.SemaphoreType.DMA((8,)),
        ],
        compiler_params=room(14),
        cost_estimate=cost(4 * coefs * depth * (feats + outs), acts, coeff, out, *pieces),
    )(where, acts, coeff, high, low, *pieces)


def residual_kernel(
    scale, where_ref, acts_ref, part_ref, coeff_ref, high_ref, low_ref, p0_ref, p1_ref, p2_ref, p3_ref,
    *refs,
):
    outs, (acts_block, grad_block, part_block, sems) = refs[:SIDE], refs[SIDE:]
    x = where_ref[0]
    depth = grad_block.shape[0]
    copies = rows_in_order(where_ref, (p0_ref, p1_ref, p2_ref, p3_ref), grad_block, sems)
    copies.append(
        pltpu.make_async_copy(acts_columns(where_ref, 2, acts_ref, depth), acts_block, sems.at[6])
    )
    copies.append(pltpu.make_async_copy(part_ref, part_block, sems.at[7]))
    for copy in copies:
        copy.start()
    basis = (high_ref[...], low_ref[...])
    kept = dot_parts(two_parts(coeff_ref[...]), basis, ((1,), (1,)))
    for copy in copies:
        copy.wait()
    term = jnp.dot(acts_block[...], grad_block[...], preferred_element_type=jnp.float32)
    part_block[...] = (part_block[...] + term * scale) - kept
    rows = outs[0].shape[0]
    for shift, out_ref in enumerate(outs):
        at = pl.multiple_of(lax.rem(x + shift, SIDE) * rows, rows)
        out_ref[...] = part_block[pl.ds(at, rows), :].astype(jnp.bfloat16)


def residual(scale, where, acts, part, coeff, high, low, pieces):
    feats, outs = part.shape
    depth = acts.shape[1] // SIDE
    fresh = jax.ShapeDtypeStruct((feats // SIDE, outs), jnp.bfloat16)
    return pl.pallas_call(
        lambda *refs: residual_kernel(scale, *refs),
        in_specs=[SMEM] + [HBM] * 2 + [VMEM] * 3 + [HBM] * len(pieces),
        out_specs=[VMEM] * SIDE,
        out_shape=[fresh] * SIDE,
        scratch_shapes=[
            pltpu.VMEM((feats, depth), jnp.bfloat16),
            pltpu.VMEM((depth, outs), jnp.bfloat16),
            pltpu.VMEM(part.shape, part.dtype),
            pltpu.SemaphoreType.DMA((8,)),
        ],
        compiler_params=room(60),
        cost_estimate=cost(feats * outs * (2 * depth + 960), part, coeff, *[fresh] * SIDE),
    )(where, acts, part, coeff, high, low, *pieces)


def finish_kernel(replicas, where_ref, total_ref, high_ref, low_ref, *refs):
    pieces, (update_ref, fresh_ref) = refs[:SIDE], refs[SIDE:]
    x = where_ref[0]
    rows, width = pieces[0].shape
    coefs = high_ref.shape[1]
    basis = (high_ref[...], low_ref[...])
    for q, piece_ref in enumerate(pieces):
        at = pl.multiple_of(lax.rem(x + SIDE - q, SIDE) * width, width)
        fresh_ref[:, pl.ds(at, width)] = piece_ref[...]
        quarters = []
        for ylo in range(2):
            for core in range(2):
                tiles = jnp.concatenate([total_ref[core, ylo, q, 0], total_ref[core, ylo, q, 1]], 0)
                quarters.append(unpacked(tiles, rows // 4, coefs))
        mean = two_parts(jnp.concatenate(quarters, 0) / replicas)
        update_ref[:, q * width : (q + 1) * width] = dot_parts(mean, basis, ((1,), (1,))).astype(
            jnp.bfloat16
        )


def finish(replicas, where, total, high, low, pieces):
    rows, width = pieces[0].shape
    out = jax.ShapeDtypeStruct((rows, SIDE * width), jnp.bfloat16)
    return pl.pallas_call(
        lambda *refs: finish_kernel(replicas, *refs),
        in_specs=[SMEM] + [VMEM] * (3 + SIDE),
        out_specs=[VMEM] * 2,
        out_shape=[out, out],
        compiler_params=room(8),
        cost_estimate=cost(6 * total.size * width, total, out, out, out),
    )(where, total, high, low, *pieces)


def shifted(x, axis, by):
    return lax.ppermute(x, axis, [(i, (i + by) % SIDE) for i in range(SIDE)])


def per_device(attn_out, out_grad, momentum, kept):
    replicas = 32
    scale = 1.0 / math.sqrt(attn_out.shape[0])
    toks, width = out_grad.shape
    where = jnp.stack([lax.axis_index("x"), lax.axis_index("yhi")]).astype(jnp.int32)

    acts = lax.all_gather(attn_out.T, "x", axis=0, tiled=True)
    first = quarter(where, out_grad)
    up, down = [shifted(first, "yhi", 1)], [shifted(first, "yhi", -1)]
    every = lax.all_to_all(pack(out_grad), "x", 0, 0, tiled=True)
    every, up[0], down[0] = lax.optimization_barrier((every, up[0], down[0]))
    rest = others(where, every)
    stored, rest = lax.optimization_barrier((momentum[0], rest))
    mom = lax.all_to_all(pack(stored, 60), "x", 0, 0, tiled=True).reshape(SIDE * toks, width // SIDE)
    own = [first, rest]
    up.append(shifted(rest, "yhi", 1))
    down.append(shifted(rest, "yhi", -1))
    over = []
    for above, below in zip(up, down):
        middle = above.shape[0] // 2
        over.append(shifted(above[:middle], "yhi", 1))
        over.append(shifted(below[middle:], "yhi", -1))

    table = basis_table(jnp.tile(kept, width // SIDE // GROUP))
    part, coeff, high, low = near(scale, where, acts, mom, table, own + up + down, 20)
    coeff, pieces = far(scale, where, acts, coeff, high, low, over)
    fresh = residual(scale, where, acts, part, coeff, high, low, over)

    tile = pieces.shape[1:]
    pieces = lax.all_to_all(pieces, ("x", "ylo", "core"), 0, 0, tiled=True)
    summed = pieces.reshape(4, 4, *tile).sum(1)
    tile = (tile[0] // 2, tile[1])
    summed, *fresh = lax.optimization_barrier((summed, *fresh))
    pieces = lax.all_to_all(summed.reshape(8, *tile), "z", 0, 0, tiled=True)
    summed = pieces.sum(0)
    spread = jnp.broadcast_to(summed[None], (16, *tile))
    spread = lax.all_to_all(spread, ("ylo", "z"), 0, 0, tiled=True)
    total = lax.all_gather(spread, "core", axis=0).reshape(2, 2, 4, 2, *tile)
    fresh = [fresh[0]] + [shifted(fresh[s], "x", s) for s in (1, 2, 3)]
    update, new_momentum = finish(
        replicas, where, total, high, low, fresh
    )
    return update, new_momentum[None]


def solution(mesh):
    fine = Mesh(mesh.devices.reshape(2, 8, 2, 4, 4), ("ylo", "z", "core", "yhi", "x"))
    return jax.shard_map(
        per_device,
        mesh=fine,
        in_specs=(P(REP, FSDP), P(REP + FSDP, None), P(REP, FSDP, None), P()),
        out_specs=(P(FSDP, None), P(REP, FSDP, None)),
        check_vma=False,
    )
```

```python
import math

import jax
import jax.numpy as jnp
from jax import lax
from jax.experimental import pallas as pl
from jax.experimental.pallas import tpu as pltpu
from jax.sharding import Mesh, PartitionSpec as P

GROUP = 64
KEEP = 16
BETA = 0.999
SIDE = 4
STEPS = 2
LANES = 128

REP = ("ylo", "z", "core")
FSDP = ("yhi", "x")

SMEM = pl.BlockSpec(memory_space=pltpu.SMEM)
VMEM = pl.BlockSpec(memory_space=pltpu.VMEM)
HBM = pl.BlockSpec(memory_space=pltpu.HBM)


def room(mebibytes):
    return pltpu.CompilerParams(vmem_limit_bytes=mebibytes * 1024 * 1024)


def basis_table(kept):
    freq = kept.astype(jnp.float32)
    points = jnp.arange(GROUP, dtype=jnp.float32) + 0.5
    weight = jnp.where(kept == 0, math.sqrt(1.0 / GROUP), math.sqrt(2.0 / GROUP)).astype(
        jnp.float32
    )
    return weight[None, :] * jnp.cos(math.pi * points[:, None] * freq[None, :] / GROUP)


def cost(flops, *arrays):
    return pl.CostEstimate(
        flops=flops, bytes_accessed=sum(a.size * a.dtype.itemsize for a in arrays), transcendentals=0
    )


def two_parts(x):
    high = x.astype(jnp.bfloat16)
    return high, (x - high.astype(jnp.float32)).astype(jnp.bfloat16)


def dot_parts(a, b, dims):
    def one(x, y):
        return lax.dot_general(x, y, (dims, ((), ())), preferred_element_type=jnp.float32)

    return one(a[0], b[0]) + (one(a[0], b[1]) + one(a[1], b[0]))


def quarter_kernel(where_ref, grad_ref, up_ref, down_ref):
    rows, width = up_ref.shape
    half = rows // 2
    at = pl.multiple_of(where_ref[0] * width, width)
    up_ref[...] = grad_ref[:, pl.ds(at, width)]
    down_ref[:half] = grad_ref[half:, pl.ds(at, width)]
    down_ref[half:] = grad_ref[:half, pl.ds(at, width)]


def quarter(where, whole):
    rows, width = whole.shape
    out = jax.ShapeDtypeStruct((rows, width // SIDE), whole.dtype)
    return pl.pallas_call(
        quarter_kernel,
        in_specs=[SMEM, VMEM],
        out_specs=[VMEM] * 2,
        out_shape=[out] * 2,
        compiler_params=room(4),
        cost_estimate=cost(0, out, out),
    )(where, whole)


def pack_kernel(whole_ref, out_ref):
    width = out_ref.shape[2]
    for q in range(SIDE):
        out_ref[q] = whole_ref[:, q * width : (q + 1) * width]


def pack(whole, weight=1):
    rows, width = whole.shape
    out = jax.ShapeDtypeStruct((SIDE, rows, width // SIDE), whole.dtype)
    return pl.pallas_call(
        pack_kernel,
        in_specs=[VMEM],
        out_specs=VMEM,
        out_shape=out,
        compiler_params=room(4),
        cost_estimate=cost(0, *[out] * weight),
    )(whole)


def others_kernel(where_ref, all_ref, up_ref, down_ref):
    rows = all_ref.shape[1]
    half = rows // 2
    one, two, three = [lax.rem(where_ref[0] + n, SIDE) for n in (1, 2, 3)]
    up_ref[:rows] = down_ref[rows + half : 2 * rows + half] = all_ref[one]
    up_ref[rows : 2 * rows] = all_ref[two]
    up_ref[2 * rows :] = down_ref[half : rows + half] = all_ref[three]
    down_ref[:half] = all_ref[two, half:]
    down_ref[2 * rows + half :] = all_ref[two, :half]


def others(where, every):
    _, toks, width = every.shape
    out = jax.ShapeDtypeStruct(((SIDE - 1) * toks, width), every.dtype)
    return pl.pallas_call(
        others_kernel,
        in_specs=[SMEM, VMEM],
        out_specs=[VMEM] * 2,
        out_shape=[out] * 2,
        compiler_params=room(8),
        cost_estimate=cost(0, every, every),
    )(where, every)


def halves_swapped(ref):
    half = ref.shape[0] // 2
    return [ref.at[half : 2 * half], ref.at[:half]]


def rows_in_order(where_ref, piece_refs, block, sems):
    each = block.shape[0] // SIDE
    copies = []
    row = 0
    for piece_ref in piece_refs:
        start = row
        while row < start + piece_ref.shape[0]:
            n, skip = divmod(row, each)
            size = min(each - skip, start + piece_ref.shape[0] - row)
            at = pl.multiple_of(lax.rem(where_ref[0] + n, SIDE) * each + skip, each // 2)
            copies.append(
                pltpu.make_async_copy(
                    piece_ref.at[row - start : row - start + size], block.at[pl.ds(at, size)], sems.at[len(copies)]
                )
            )
            row += size
    return copies


def acts_columns(where_ref, shift, acts_ref, depth):
    at = lax.rem(where_ref[1] + shift, SIDE) * depth
    return acts_ref.at[:, pl.ds(pl.multiple_of(at, depth), depth)]


def near_kernel(scale, where_ref, acts_ref, mom_ref, table_ref, *rest):
    pieces, rest = rest[:6], rest[6:]
    part_ref, coeff_ref, high_ref, low_ref, grad_block, sems = rest
    depth = grad_block.shape[0] // 3

    @pl.when(pl.program_id(0) == 0)
    def _():
        copies = []
        own, up, down = pieces[:2], pieces[2:4], pieces[4:]
        down = [*halves_swapped(down[0]), *halves_swapped(down[1])]
        for n, refs in enumerate((own, up, down)):
            block = grad_block.at[n * depth : (n + 1) * depth]
            copies += rows_in_order(where_ref, refs, block, sems.at[n])
        for copy in copies:
            copy.start()
        rows, coefs = high_ref.shape
        table = jnp.concatenate([table_ref[...]] * (rows // GROUP), 0)
        row = lax.broadcasted_iota(jnp.int32, (rows, coefs), 0) // GROUP
        col = lax.broadcasted_iota(jnp.int32, (rows, coefs), 1) // KEEP
        high_ref[...], low_ref[...] = two_parts(jnp.where(row == col, table, 0.0))
        for copy in copies:
            copy.wait()

    total = None
    for n, shift in enumerate((0, 3, 1)):
        at = pl.multiple_of(lax.rem(where_ref[1] + shift, SIDE) * depth, depth)
        term = jnp.dot(
            acts_ref[:, pl.ds(at, depth)], grad_block[n * depth : (n + 1) * depth],
            preferred_element_type=jnp.float32,
        )
        total = term if total is None else total + term
    part = BETA * mom_ref[...].astype(jnp.float32) + total * scale
    part_ref[...] = part
    coeff_ref[...] = dot_parts(two_parts(part), (high_ref[...], low_ref[...]), ((1,), (0,)))


def near(scale, where, acts, mom, table, pieces, weight=1):
    feats, toks = acts.shape
    rows = feats // STEPS
    outs = pieces[0].shape[1]
    coefs = table.shape[1]
    part = jax.ShapeDtypeStruct((feats, outs), jnp.float32)
    coeff = jax.ShapeDtypeStruct((feats, coefs), jnp.float32)
    basis = jax.ShapeDtypeStruct((outs, coefs), jnp.bfloat16)
    some = pl.BlockSpec((rows, outs), lambda p, w: (p, 0))
    whole = pl.BlockSpec(basis.shape, lambda p, w: (0, 0))
    return pl.pallas_call(
        lambda *refs: near_kernel(scale, *refs),
        grid_spec=pltpu.PrefetchScalarGridSpec(
            num_scalar_prefetch=1,
            grid=(STEPS,),
            in_specs=[
                pl.BlockSpec((rows, toks), lambda p, w: (p, 0)),
                some,
                pl.BlockSpec(table.shape, lambda p, w: (0, 0)),
                *[HBM] * len(pieces),
            ],
            out_specs=[some, pl.BlockSpec((rows, coefs), lambda p, w: (p, 0)), whole, whole],
            scratch_shapes=[
                pltpu.VMEM((3 * toks // SIDE, outs), jnp.bfloat16),
                pltpu.SemaphoreType.DMA((3, 6)),
            ],
        ),
        out_shape=[part, coeff, basis, basis],
        compiler_params=room(60),
        cost_estimate=cost(weight * 3 * feats * toks * outs // 2, acts, part, *pieces),
    )(where, acts, mom, table, *pieces)


def packed(coeff, rows):
    wide = coeff.shape[1] - LANES
    rest = [coeff[n : n + 8, LANES:] for n in range(0, coeff.shape[0], 8)]
    rest += [jnp.zeros_like(rest[0])] * (-len(rest) % (LANES // wide))
    tiles = [
        jnp.concatenate(rest[n : n + LANES // wide], 1) for n in range(0, len(rest), LANES // wide)
    ]
    blank = jnp.zeros((rows - coeff.shape[0] - 8 * len(tiles), LANES), coeff.dtype)
    return jnp.concatenate([coeff[:, :LANES], *tiles, blank], 0)


def unpacked(tiles, rows, coefs):
    wide = coefs - LANES
    rest = []
    for n in range(rows // 8):
        row, lane = rows + 8 * (n // (LANES // wide)), wide * (n % (LANES // wide))
        rest.append(tiles[row : row + 8, lane : lane + wide])
    return jnp.concatenate([tiles[:rows], jnp.concatenate(rest, 0)], 1)


def far_kernel(
    scale, where_ref, acts_ref, near_ref, high_ref, low_ref, p0_ref, p1_ref, p2_ref, p3_ref,
    packed_ref, acts_block, grad_block, near_block, high_block, low_block, sems,
):
    depth = grad_block.shape[0]
    copies = rows_in_order(where_ref, (p0_ref, p1_ref, p2_ref, p3_ref), grad_block, sems)
    copies.append(pltpu.make_async_copy(high_ref, high_block, sems.at[8]))
    copies.append(pltpu.make_async_copy(low_ref, low_block, sems.at[9]))
    last = [
        pltpu.make_async_copy(
            acts_columns(where_ref, 2, acts_ref, depth), acts_block, sems.at[6]
        ),
        pltpu.make_async_copy(near_ref, near_block, sems.at[7]),
    ]
    for copy in copies + last:
        copy.start()
    for copy in copies:
        copy.wait()

    def dot(a, b):
        return jnp.dot(a, b, preferred_element_type=jnp.float32)

    grad = grad_block[...]
    high, low = two_parts(dot(grad, high_block[...]) + dot(grad, low_block[...]))
    for copy in last:
        copy.wait()
    acts = acts_block[...]
    coeff = near_block[...] + (dot(acts, high) + dot(acts, low)) * scale
    count, rows, _ = packed_ref.shape
    each = coeff.shape[0] // count
    for n in range(count):
        packed_ref[n] = packed(coeff[n * each : (n + 1) * each], rows)


def far(scale, where, acts, coeff, high, low, pieces):
    outs, coefs = high.shape
    feats = acts.shape[0]
    depth = acts.shape[1] // SIDE
    out = jax.ShapeDtypeStruct((16, 64, LANES), jnp.float32)
    return pl.pallas_call(
        lambda *refs: far_kernel(scale, *refs),
        in_specs=[SMEM] + [HBM] * (4 + len(pieces)),
        out_specs=VMEM,
        out_shape=out,
        scratch_shapes=[
            pltpu.VMEM((feats, depth), jnp.bfloat16),
            pltpu.VMEM((depth, outs), jnp.bfloat16),
            pltpu.VMEM(coeff.shape, coeff.dtype),
            pltpu.VMEM(high.shape, high.dtype),
            pltpu.VMEM(low.shape, low.dtype),
            pltpu.SemaphoreType.DMA((10,)),
        ],
        compiler_params=room(60),
        cost_estimate=cost(4 * coefs * depth * (feats + outs), acts, coeff, out, *pieces),
    )(where, acts, coeff, high, low, *pieces)


def residual_kernel(
    scale, where_ref, acts_ref, part_ref, packed_ref, high_ref, low_ref, p0_ref, p1_ref, p2_ref, p3_ref,
    *refs,
):
    outs, (acts_block, grad_block, part_block, sems) = refs[:SIDE], refs[SIDE:]
    x = where_ref[0]
    depth = grad_block.shape[0]
    copies = rows_in_order(where_ref, (p0_ref, p1_ref, p2_ref, p3_ref), grad_block, sems)
    copies.append(
        pltpu.make_async_copy(acts_columns(where_ref, 2, acts_ref, depth), acts_block, sems.at[6])
    )
    copies.append(pltpu.make_async_copy(part_ref, part_block, sems.at[7]))
    for copy in copies:
        copy.start()
    basis = (high_ref[...], low_ref[...])
    count = packed_ref.shape[0]
    each, coefs = part_block.shape[0] // count, high_ref.shape[1]
    coeff = jnp.concatenate([unpacked(packed_ref[n], each, coefs) for n in range(count)], 0)
    kept = dot_parts(two_parts(coeff), basis, ((1,), (1,)))
    for copy in copies:
        copy.wait()
    term = jnp.dot(acts_block[...], grad_block[...], preferred_element_type=jnp.float32)
    part_block[...] = (part_block[...] + term * scale) - kept
    rows = outs[0].shape[0]
    for shift, out_ref in enumerate(outs):
        at = pl.multiple_of(lax.rem(x + shift, SIDE) * rows, rows)
        out_ref[...] = part_block[pl.ds(at, rows), :].astype(jnp.bfloat16)


def residual(scale, where, acts, part, coeff, high, low, pieces):
    feats, outs = part.shape
    depth = acts.shape[1] // SIDE
    fresh = jax.ShapeDtypeStruct((feats // SIDE, outs), jnp.bfloat16)
    return pl.pallas_call(
        lambda *refs: residual_kernel(scale, *refs),
        in_specs=[SMEM] + [HBM] * 2 + [VMEM] * 3 + [HBM] * len(pieces),
        out_specs=[VMEM] * SIDE,
        out_shape=[fresh] * SIDE,
        scratch_shapes=[
            pltpu.VMEM((feats, depth), jnp.bfloat16),
            pltpu.VMEM((depth, outs), jnp.bfloat16),
            pltpu.VMEM(part.shape, part.dtype),
            pltpu.SemaphoreType.DMA((8,)),
        ],
        compiler_params=room(60),
        cost_estimate=cost(feats * outs * (2 * depth + 960), part, coeff, *[fresh] * SIDE),
    )(where, acts, part, coeff, high, low, *pieces)


def decode_kernel(replicas, total_ref, high_ref, low_ref, update_ref):
    rows = update_ref.shape[0]
    width, coefs = high_ref.shape
    basis = (high_ref[...], low_ref[...])
    for q in range(SIDE):
        quarters = []
        for ylo in range(2):
            for core in range(2):
                tiles = jnp.concatenate([total_ref[core, ylo, q, 0], total_ref[core, ylo, q, 1]], 0)
                quarters.append(unpacked(tiles, rows // 4, coefs))
        mean = two_parts(jnp.concatenate(quarters, 0) / replicas)
        update_ref[:, q * width : (q + 1) * width] = dot_parts(mean, basis, ((1,), (1,))).astype(
            jnp.bfloat16
        )


def decode(replicas, rows, total, high, low):
    out = jax.ShapeDtypeStruct((rows, SIDE * high.shape[0]), jnp.bfloat16)
    return pl.pallas_call(
        lambda *refs: decode_kernel(replicas, *refs),
        in_specs=[VMEM] * 3,
        out_specs=VMEM,
        out_shape=out,
        compiler_params=room(8),
        cost_estimate=cost(6 * total.size * high.shape[0], total, out),
    )(total, high, low)


def columns_kernel(where_ref, *refs):
    *pieces, out_ref = refs
    width = pieces[0].shape[1]
    for n, piece_ref in enumerate(pieces):
        at = lax.rem(where_ref[0] + SIDE - n, SIDE) * width
        out_ref[:, pl.ds(pl.multiple_of(at, width), width)] = piece_ref[...]


def columns(where, pieces):
    rows, width = pieces[0].shape
    out = jax.ShapeDtypeStruct((rows, SIDE * width), pieces[0].dtype)
    return pl.pallas_call(
        columns_kernel,
        in_specs=[SMEM] + [VMEM] * SIDE,
        out_specs=VMEM,
        out_shape=out,
        compiler_params=room(4),
        cost_estimate=cost(0, out, out),
    )(where, *pieces)


def shifted(x, axis, by):
    return lax.ppermute(x, axis, [(i, (i + by) % SIDE) for i in range(SIDE)])


def per_device(attn_out, out_grad, momentum, kept):
    replicas = 32
    scale = 1.0 / math.sqrt(attn_out.shape[0])
    toks, width = out_grad.shape
    where = jnp.stack([lax.axis_index("x"), lax.axis_index("yhi")]).astype(jnp.int32)

    acts = lax.all_gather(attn_out.T, "x", axis=0, tiled=True)
    first, swapped = quarter(where, out_grad)
    up, down = [shifted(first, "yhi", 1)], [shifted(swapped, "yhi", -1)]
    every = lax.all_to_all(pack(out_grad), "x", 0, 0, tiled=True)
    every, up[0], down[0] = lax.optimization_barrier((every, up[0], down[0]))
    rest, swapped = others(where, every)
    stored, rest, swapped = lax.optimization_barrier((momentum[0], rest, swapped))
    mom = lax.all_to_all(pack(stored, 60), "x", 0, 0, tiled=True).reshape(SIDE * toks, width // SIDE)
    own = [first, rest]
    up.append(shifted(rest, "yhi", 1))
    down.append(shifted(swapped, "yhi", -1))
    over = []
    for above, below in zip(up, down):
        middle = above.shape[0] // 2
        over.append(shifted(above[:middle], "yhi", 1))
        over.append(shifted(below[:middle], "yhi", -1))

    table = basis_table(jnp.tile(kept, width // SIDE // GROUP))
    part, coeff, high, low = near(scale, where, acts, mom, table, own + up + down, 20)
    pieces = far(scale, where, acts, coeff, high, low, over)
    fresh = residual(scale, where, acts, part, pieces, high, low, over)

    tile = pieces.shape[1:]
    pieces = lax.all_to_all(pieces, ("x", "ylo", "core"), 0, 0, tiled=True)
    summed = pieces.reshape(4, 4, *tile).sum(1)
    tile = (tile[0] // 2, tile[1])
    summed, *fresh = lax.optimization_barrier((summed, *fresh))
    pieces = lax.all_to_all(summed.reshape(8, *tile), "z", 0, 0, tiled=True)
    summed = pieces.sum(0)
    spread = jnp.broadcast_to(summed[None], (16, *tile))
    spread = lax.all_to_all(spread, ("ylo", "z"), 0, 0, tiled=True)
    total = lax.all_gather(spread, "core", axis=0).reshape(2, 2, 4, 2, *tile)
    fresh = [fresh[0]] + [shifted(fresh[s], "x", s) for s in (1, 2, 3)]
    update = decode(replicas, toks, total, high, low)
    total, *fresh = lax.optimization_barrier((total, *fresh))
    new_momentum = columns(where, fresh)
    return update, new_momentum[None]


def solution(mesh):
    fine = Mesh(mesh.devices.reshape(2, 8, 2, 4, 4), ("ylo", "z", "core", "yhi", "x"))
    return jax.shard_map(
        per_device,
        mesh=fine,
        in_specs=(P(REP, FSDP), P(REP + FSDP, None), P(REP, FSDP, None), P()),
        out_specs=(P(FSDP, None), P(REP, FSDP, None)),
        check_vma=False,
    )
```

```python
import math

import jax
import jax.numpy as jnp
from jax import lax
from jax.experimental import pallas as pl
from jax.experimental.pallas import tpu as pltpu
from jax.sharding import Mesh, PartitionSpec as P

GROUP = 64
KEEP = 16
BETA = 0.999
SIDE = 4
STEPS = 2
LANES = 128

REP = ("ylo", "z", "core")
FSDP = ("yhi", "x")

SMEM = pl.BlockSpec(memory_space=pltpu.SMEM)
VMEM = pl.BlockSpec(memory_space=pltpu.VMEM)
HBM = pl.BlockSpec(memory_space=pltpu.HBM)


def room(mebibytes):
    return pltpu.CompilerParams(vmem_limit_bytes=mebibytes * 1024 * 1024)


def basis_table(kept):
    freq = kept.astype(jnp.float32)
    points = jnp.arange(GROUP, dtype=jnp.float32) + 0.5
    weight = jnp.where(kept == 0, math.sqrt(1.0 / GROUP), math.sqrt(2.0 / GROUP)).astype(
        jnp.float32
    )
    return weight[None, :] * jnp.cos(math.pi * points[:, None] * freq[None, :] / GROUP)


def cost(flops, *arrays):
    return pl.CostEstimate(
        flops=flops, bytes_accessed=sum(a.size * a.dtype.itemsize for a in arrays), transcendentals=0
    )


def two_parts(x):
    high = x.astype(jnp.bfloat16)
    return high, (x - high.astype(jnp.float32)).astype(jnp.bfloat16)


def dot_parts(a, b, dims):
    def one(x, y):
        return lax.dot_general(x, y, (dims, ((), ())), preferred_element_type=jnp.float32)

    return one(a[0], b[0]) + (one(a[0], b[1]) + one(a[1], b[0]))


def quarter_kernel(where_ref, grad_ref, up_ref, down_ref):
    rows, width = up_ref.shape
    half = rows // 2
    at = pl.multiple_of(where_ref[0] * width, width)
    up_ref[...] = grad_ref[:, pl.ds(at, width)]
    down_ref[:half] = grad_ref[half:, pl.ds(at, width)]
    down_ref[half:] = grad_ref[:half, pl.ds(at, width)]


def quarter(where, whole):
    rows, width = whole.shape
    out = jax.ShapeDtypeStruct((rows, width // SIDE), whole.dtype)
    return pl.pallas_call(
        quarter_kernel,
        in_specs=[SMEM, VMEM],
        out_specs=[VMEM] * 2,
        out_shape=[out] * 2,
        compiler_params=room(4),
        cost_estimate=cost(0, out, out),
    )(where, whole)


def pack_kernel(whole_ref, out_ref):
    width = out_ref.shape[2]
    for q in range(SIDE):
        out_ref[q] = whole_ref[:, q * width : (q + 1) * width]


def pack(whole, weight=1):
    rows, width = whole.shape
    out = jax.ShapeDtypeStruct((SIDE, rows, width // SIDE), whole.dtype)
    return pl.pallas_call(
        pack_kernel,
        in_specs=[VMEM],
        out_specs=VMEM,
        out_shape=out,
        compiler_params=room(4),
        cost_estimate=cost(0, *[out] * weight),
    )(whole)


def others_kernel(where_ref, all_ref, up_ref, down_ref):
    rows = all_ref.shape[1]
    half = rows // 2
    one, two, three = [lax.rem(where_ref[0] + n, SIDE) for n in (1, 2, 3)]
    up_ref[:rows] = down_ref[rows + half : 2 * rows + half] = all_ref[one]
    up_ref[rows : 2 * rows] = all_ref[two]
    up_ref[2 * rows :] = down_ref[half : rows + half] = all_ref[three]
    down_ref[:half] = all_ref[two, half:]
    down_ref[2 * rows + half :] = all_ref[two, :half]


def others(where, every):
    _, toks, width = every.shape
    out = jax.ShapeDtypeStruct(((SIDE - 1) * toks, width), every.dtype)
    return pl.pallas_call(
        others_kernel,
        in_specs=[SMEM, VMEM],
        out_specs=[VMEM] * 2,
        out_shape=[out] * 2,
        compiler_params=room(8),
        cost_estimate=cost(0, every, every),
    )(where, every)


def halves_swapped(ref):
    half = ref.shape[0] // 2
    return [ref.at[half : 2 * half], ref.at[:half]]


def rows_in_order(where_ref, piece_refs, block, sems):
    each = block.shape[0] // SIDE
    copies = []
    row = 0
    for piece_ref in piece_refs:
        start = row
        while row < start + piece_ref.shape[0]:
            n, skip = divmod(row, each)
            size = min(each - skip, start + piece_ref.shape[0] - row)
            at = pl.multiple_of(lax.rem(where_ref[0] + n, SIDE) * each + skip, each // 2)
            copies.append(
                pltpu.make_async_copy(
                    piece_ref.at[row - start : row - start + size], block.at[pl.ds(at, size)], sems.at[len(copies)]
                )
            )
            row += size
    return copies


def acts_columns(where_ref, shift, acts_ref, depth):
    at = lax.rem(where_ref[1] + shift, SIDE) * depth
    return acts_ref.at[:, pl.ds(pl.multiple_of(at, depth), depth)]


def near_kernel(scale, where_ref, acts_ref, mom_ref, table_ref, *rest):
    pieces, rest = rest[:6], rest[6:]
    part_ref, coeff_ref, high_ref, low_ref, grad_block, sems = rest
    depth = grad_block.shape[0] // 3

    @pl.when(pl.program_id(0) == 0)
    def _():
        copies = []
        own, up, down = pieces[:2], pieces[2:4], pieces[4:]
        down = [*halves_swapped(down[0]), *halves_swapped(down[1])]
        for n, refs in enumerate((own, up, down)):
            block = grad_block.at[n * depth : (n + 1) * depth]
            copies += rows_in_order(where_ref, refs, block, sems.at[n])
        for copy in copies:
            copy.start()
        rows, coefs = high_ref.shape
        table = jnp.concatenate([table_ref[...]] * (rows // GROUP), 0)
        row = lax.broadcasted_iota(jnp.int32, (rows, coefs), 0) // GROUP
        col = lax.broadcasted_iota(jnp.int32, (rows, coefs), 1) // KEEP
        high_ref[...], low_ref[...] = two_parts(jnp.where(row == col, table, 0.0))
        for copy in copies:
            copy.wait()

    total = None
    ylo = where_ref[2]
    for n, shift in enumerate((0, 3 - 2 * ylo, 1 + 2 * ylo)):
        at = pl.multiple_of(lax.rem(where_ref[1] + shift, SIDE) * depth, depth)
        term = jnp.dot(
            acts_ref[:, pl.ds(at, depth)], grad_block[n * depth : (n + 1) * depth],
            preferred_element_type=jnp.float32,
        )
        total = term if total is None else total + term
    part = BETA * mom_ref[...].astype(jnp.float32) + total * scale
    part_ref[...] = part
    coeff_ref[...] = dot_parts(two_parts(part), (high_ref[...], low_ref[...]), ((1,), (0,)))


def near(scale, where, acts, mom, table, pieces, weight=1):
    feats, toks = acts.shape
    rows = feats // STEPS
    outs = pieces[0].shape[1]
    coefs = table.shape[1]
    part = jax.ShapeDtypeStruct((feats, outs), jnp.float32)
    coeff = jax.ShapeDtypeStruct((feats, coefs), jnp.float32)
    basis = jax.ShapeDtypeStruct((outs, coefs), jnp.bfloat16)
    some = pl.BlockSpec((rows, outs), lambda p, w: (p, 0))
    whole = pl.BlockSpec(basis.shape, lambda p, w: (0, 0))
    return pl.pallas_call(
        lambda *refs: near_kernel(scale, *refs),
        grid_spec=pltpu.PrefetchScalarGridSpec(
            num_scalar_prefetch=1,
            grid=(STEPS,),
            in_specs=[
                pl.BlockSpec((rows, toks), lambda p, w: (p, 0)),
                some,
                pl.BlockSpec(table.shape, lambda p, w: (0, 0)),
                *[HBM] * len(pieces),
            ],
            out_specs=[some, pl.BlockSpec((rows, coefs), lambda p, w: (p, 0)), whole, whole],
            scratch_shapes=[
                pltpu.VMEM((3 * toks // SIDE, outs), jnp.bfloat16),
                pltpu.SemaphoreType.DMA((3, 6)),
            ],
        ),
        out_shape=[part, coeff, basis, basis],
        compiler_params=room(60),
        cost_estimate=cost(weight * 3 * feats * toks * outs // 2, acts, part, *pieces),
    )(where, acts, mom, table, *pieces)


def packed(coeff, rows):
    wide = coeff.shape[1] - LANES
    rest = [coeff[n : n + 8, LANES:] for n in range(0, coeff.shape[0], 8)]
    rest += [jnp.zeros_like(rest[0])] * (-len(rest) % (LANES // wide))
    tiles = [
        jnp.concatenate(rest[n : n + LANES // wide], 1) for n in range(0, len(rest), LANES // wide)
    ]
    blank = jnp.zeros((rows - coeff.shape[0] - 8 * len(tiles), LANES), coeff.dtype)
    return jnp.concatenate([coeff[:, :LANES], *tiles, blank], 0)


def unpacked(tiles, rows, coefs):
    wide = coefs - LANES
    rest = []
    for n in range(rows // 8):
        row, lane = rows + 8 * (n // (LANES // wide)), wide * (n % (LANES // wide))
        rest.append(tiles[row : row + 8, lane : lane + wide])
    return jnp.concatenate([tiles[:rows], jnp.concatenate(rest, 0)], 1)


def far_kernel(
    scale, where_ref, acts_ref, near_ref, high_ref, low_ref, p0_ref, p1_ref, p2_ref, p3_ref,
    packed_ref, acts_block, grad_block, near_block, high_block, low_block, sems,
):
    depth = grad_block.shape[0]
    copies = rows_in_order(where_ref, (p0_ref, p1_ref, p2_ref, p3_ref), grad_block, sems)
    copies.append(pltpu.make_async_copy(high_ref, high_block, sems.at[8]))
    copies.append(pltpu.make_async_copy(low_ref, low_block, sems.at[9]))
    last = [
        pltpu.make_async_copy(
            acts_columns(where_ref, 2, acts_ref, depth), acts_block, sems.at[6]
        ),
        pltpu.make_async_copy(near_ref, near_block, sems.at[7]),
    ]
    for copy in copies + last:
        copy.start()
    for copy in copies:
        copy.wait()

    def dot(a, b):
        return jnp.dot(a, b, preferred_element_type=jnp.float32)

    grad = grad_block[...]
    high, low = two_parts(dot(grad, high_block[...]) + dot(grad, low_block[...]))
    for copy in last:
        copy.wait()
    acts = acts_block[...]
    coeff = near_block[...] + (dot(acts, high) + dot(acts, low)) * scale
    count, rows, _ = packed_ref.shape
    each = coeff.shape[0] // count
    for n in range(count):
        packed_ref[n] = packed(coeff[n * each : (n + 1) * each], rows)


def far(scale, where, acts, coeff, high, low, pieces):
    outs, coefs = high.shape
    feats = acts.shape[0]
    depth = acts.shape[1] // SIDE
    out = jax.ShapeDtypeStruct((16, 64, LANES), jnp.float32)
    return pl.pallas_call(
        lambda *refs: far_kernel(scale, *refs),
        in_specs=[SMEM] + [HBM] * (4 + len(pieces)),
        out_specs=VMEM,
        out_shape=out,
        scratch_shapes=[
            pltpu.VMEM((feats, depth), jnp.bfloat16),
            pltpu.VMEM((depth, outs), jnp.bfloat16),
            pltpu.VMEM(coeff.shape, coeff.dtype),
            pltpu.VMEM(high.shape, high.dtype),
            pltpu.VMEM(low.shape, low.dtype),
            pltpu.SemaphoreType.DMA((10,)),
        ],
        compiler_params=room(60),
        cost_estimate=cost(4 * coefs * depth * (feats + outs), acts, coeff, out, *pieces),
    )(where, acts, coeff, high, low, *pieces)


def residual_kernel(
    scale, where_ref, acts_ref, part_ref, packed_ref, high_ref, low_ref, p0_ref, p1_ref, p2_ref, p3_ref,
    *refs,
):
    outs, (acts_block, grad_block, part_block, sems) = refs[:SIDE], refs[SIDE:]
    x = where_ref[0]
    depth = grad_block.shape[0]
    copies = rows_in_order(where_ref, (p0_ref, p1_ref, p2_ref, p3_ref), grad_block, sems)
    copies.append(
        pltpu.make_async_copy(acts_columns(where_ref, 2, acts_ref, depth), acts_block, sems.at[6])
    )
    copies.append(pltpu.make_async_copy(part_ref, part_block, sems.at[7]))
    for copy in copies:
        copy.start()
    basis = (high_ref[...], low_ref[...])
    count = packed_ref.shape[0]
    each, coefs = part_block.shape[0] // count, high_ref.shape[1]
    coeff = jnp.concatenate([unpacked(packed_ref[n], each, coefs) for n in range(count)], 0)
    kept = dot_parts(two_parts(coeff), basis, ((1,), (1,)))
    for copy in copies:
        copy.wait()
    term = jnp.dot(acts_block[...], grad_block[...], preferred_element_type=jnp.float32)
    part_block[...] = (part_block[...] + term * scale) - kept
    rows = outs[0].shape[0]
    for shift, out_ref in enumerate(outs):
        at = pl.multiple_of(lax.rem(x + shift, SIDE) * rows, rows)
        out_ref[...] = part_block[pl.ds(at, rows), :].astype(jnp.bfloat16)


def residual(scale, where, acts, part, coeff, high, low, pieces):
    feats, outs = part.shape
    depth = acts.shape[1] // SIDE
    fresh = jax.ShapeDtypeStruct((feats // SIDE, outs), jnp.bfloat16)
    return pl.pallas_call(
        lambda *refs: residual_kernel(scale, *refs),
        in_specs=[SMEM] + [HBM] * 2 + [VMEM] * 3 + [HBM] * len(pieces),
        out_specs=[VMEM] * SIDE,
        out_shape=[fresh] * SIDE,
        scratch_shapes=[
            pltpu.VMEM((feats, depth), jnp.bfloat16),
            pltpu.VMEM((depth, outs), jnp.bfloat16),
            pltpu.VMEM(part.shape, part.dtype),
            pltpu.SemaphoreType.DMA((8,)),
        ],
        compiler_params=room(60),
        cost_estimate=cost(feats * outs * (2 * depth + 960), part, coeff, *[fresh] * SIDE),
    )(where, acts, part, coeff, high, low, *pieces)


def decode_kernel(replicas, total_ref, high_ref, low_ref, update_ref):
    rows = update_ref.shape[0]
    width, coefs = high_ref.shape
    basis = (high_ref[...], low_ref[...])
    for q in range(SIDE):
        quarters = []
        for ylo in range(2):
            for core in range(2):
                tiles = jnp.concatenate([total_ref[core, ylo, q, 0], total_ref[core, ylo, q, 1]], 0)
                quarters.append(unpacked(tiles, rows // 4, coefs))
        mean = two_parts(jnp.concatenate(quarters, 0) / replicas)
        update_ref[:, q * width : (q + 1) * width] = dot_parts(mean, basis, ((1,), (1,))).astype(
            jnp.bfloat16
        )


def decode(replicas, rows, total, high, low):
    out = jax.ShapeDtypeStruct((rows, SIDE * high.shape[0]), jnp.bfloat16)
    return pl.pallas_call(
        lambda *refs: decode_kernel(replicas, *refs),
        in_specs=[VMEM] * 3,
        out_specs=VMEM,
        out_shape=out,
        compiler_params=room(8),
        cost_estimate=cost(6 * total.size * high.shape[0], total, out),
    )(total, high, low)


def columns_kernel(where_ref, *refs):
    *pieces, out_ref = refs
    width = pieces[0].shape[1]
    for n, piece_ref in enumerate(pieces):
        at = lax.rem(where_ref[0] + SIDE - n, SIDE) * width
        out_ref[:, pl.ds(pl.multiple_of(at, width), width)] = piece_ref[...]


def columns(where, pieces):
    rows, width = pieces[0].shape
    out = jax.ShapeDtypeStruct((rows, SIDE * width), pieces[0].dtype)
    return pl.pallas_call(
        columns_kernel,
        in_specs=[SMEM] + [VMEM] * SIDE,
        out_specs=VMEM,
        out_shape=out,
        compiler_params=room(4),
        cost_estimate=cost(0, out, out),
    )(where, *pieces)


def y_shifted(x, by):
    pairs = []
    for ylo, step in ((0, by), (1, -by)):
        pairs += [(SIDE * ylo + i, SIDE * ylo + (i + step) % SIDE) for i in range(SIDE)]
    return lax.ppermute(x, ("ylo", "yhi"), pairs)


def shifted(x, axis, by):
    return lax.ppermute(x, axis, [(i, (i + by) % SIDE) for i in range(SIDE)])


def per_device(attn_out, out_grad, momentum, kept):
    replicas = 32
    scale = 1.0 / math.sqrt(attn_out.shape[0])
    toks, width = out_grad.shape
    where = jnp.stack([lax.axis_index(name) for name in ("x", "yhi", "ylo")]).astype(jnp.int32)

    acts = lax.all_gather(attn_out.T, "x", axis=0, tiled=True)
    first, swapped = quarter(where, out_grad)
    up, down = [y_shifted(first, 1)], [y_shifted(swapped, -1)]
    every = lax.all_to_all(pack(out_grad), "x", 0, 0, tiled=True)
    every, up[0], down[0] = lax.optimization_barrier((every, up[0], down[0]))
    rest, swapped = others(where, every)
    stored, rest, swapped = lax.optimization_barrier((momentum[0], rest, swapped))
    mom = lax.all_to_all(pack(stored, 60), "x", 0, 0, tiled=True).reshape(SIDE * toks, width // SIDE)
    own = [first, rest]
    up.append(y_shifted(rest, 1))
    down.append(y_shifted(swapped, -1))
    over = []
    for above, below in zip(up, down):
        middle = above.shape[0] // 2
        over.append(y_shifted(above[:middle], 1))
        over.append(y_shifted(below[:middle], -1))

    table = basis_table(jnp.tile(kept, width // SIDE // GROUP))
    part, coeff, high, low = near(scale, where, acts, mom, table, own + up + down, 20)
    pieces = far(scale, where, acts, coeff, high, low, over)
    fresh = residual(scale, where, acts, part, pieces, high, low, over)

    tile = pieces.shape[1:]
    pieces = lax.all_to_all(pieces, ("x", "ylo", "core"), 0, 0, tiled=True)
    summed = pieces.reshape(4, 4, *tile).sum(1)
    tile = (tile[0] // 2, tile[1])
    summed, *fresh = lax.optimization_barrier((summed, *fresh))
    pieces = lax.all_to_all(summed.reshape(8, *tile), "z", 0, 0, tiled=True)
    summed = pieces.sum(0)
    spread = jnp.broadcast_to(summed[None], (16, *tile))
    spread = lax.all_to_all(spread, ("ylo", "z"), 0, 0, tiled=True)
    total = lax.all_gather(spread, "core", axis=0).reshape(2, 2, 4, 2, *tile)
    fresh = [fresh[0]] + [shifted(fresh[s], "x", s) for s in (1, 2, 3)]
    update = decode(replicas, toks, total, high, low)
    total, *fresh = lax.optimization_barrier((total, *fresh))
    new_momentum = columns(where, fresh)
    return update, new_momentum[None]


def solution(mesh):
    fine = Mesh(mesh.devices.reshape(2, 8, 2, 4, 4), ("ylo", "z", "core", "yhi", "x"))
    return jax.shard_map(
        per_device,
        mesh=fine,
        in_specs=(P(REP, FSDP), P(REP + FSDP, None), P(REP, FSDP, None), P()),
        out_specs=(P(FSDP, None), P(REP, FSDP, None)),
        check_vma=False,
    )
```

```python
import math

import jax
import jax.numpy as jnp
from jax import lax
from jax.experimental import pallas as pl
from jax.experimental.pallas import tpu as pltpu
from jax.sharding import Mesh, PartitionSpec as P

GROUP = 64
KEEP = 16
BETA = 0.999
SIDE = 4
LANES = 128

REP = ("ylo", "z", "core")
FSDP = ("yhi", "x")

SMEM = pl.BlockSpec(memory_space=pltpu.SMEM)
VMEM = pl.BlockSpec(memory_space=pltpu.VMEM)
HBM = pl.BlockSpec(memory_space=pltpu.HBM)


def room(mebibytes):
    return pltpu.CompilerParams(vmem_limit_bytes=mebibytes * 1024 * 1024)


def basis_table(kept):
    freq = kept.astype(jnp.float32)
    points = jnp.arange(GROUP, dtype=jnp.float32) + 0.5
    weight = jnp.where(kept == 0, math.sqrt(1.0 / GROUP), math.sqrt(2.0 / GROUP)).astype(
        jnp.float32
    )
    return weight[None, :] * jnp.cos(math.pi * points[:, None] * freq[None, :] / GROUP)


def cost(flops, *arrays):
    return pl.CostEstimate(
        flops=flops, bytes_accessed=sum(a.size * a.dtype.itemsize for a in arrays), transcendentals=0
    )


def two_parts(x):
    high = x.astype(jnp.bfloat16)
    return high, (x - high.astype(jnp.float32)).astype(jnp.bfloat16)


def dot_parts(a, b, dims):
    def one(x, y):
        return lax.dot_general(x, y, (dims, ((), ())), preferred_element_type=jnp.float32)

    return one(a[0], b[0]) + (one(a[0], b[1]) + one(a[1], b[0]))


def quarter_kernel(where_ref, grad_ref, up_ref, down_ref):
    rows, width = up_ref.shape
    half = rows // 2
    at = pl.multiple_of(where_ref[0] * width, width)
    up_ref[...] = grad_ref[:, pl.ds(at, width)]
    down_ref[:half] = grad_ref[half:, pl.ds(at, width)]
    down_ref[half:] = grad_ref[:half, pl.ds(at, width)]


def quarter(where, whole):
    rows, width = whole.shape
    out = jax.ShapeDtypeStruct((rows, width // SIDE), whole.dtype)
    return pl.pallas_call(
        quarter_kernel,
        in_specs=[SMEM, VMEM],
        out_specs=[VMEM] * 2,
        out_shape=[out] * 2,
        compiler_params=room(4),
        cost_estimate=cost(0, out, out),
    )(where, whole)


def pack_kernel(whole_ref, out_ref):
    width = out_ref.shape[2]
    for q in range(SIDE):
        out_ref[q] = whole_ref[:, q * width : (q + 1) * width]


def pack(whole, weight=1):
    rows, width = whole.shape
    out = jax.ShapeDtypeStruct((SIDE, rows, width // SIDE), whole.dtype)
    return pl.pallas_call(
        pack_kernel,
        in_specs=[VMEM],
        out_specs=VMEM,
        out_shape=out,
        compiler_params=room(4),
        cost_estimate=cost(0, *[out] * weight),
    )(whole)


def pack_through_kernel(whole_ref, out_ref, block, sems):
    width = out_ref.shape[2]
    reads, writes = [], []
    for q in range(SIDE):
        span = slice(q * width, (q + 1) * width)
        reads.append(pltpu.make_async_copy(whole_ref.at[:, span], block.at[q], sems.at[0, q]))
        writes.append(pltpu.make_async_copy(block.at[q], out_ref.at[q], sems.at[1, q]))
    for copy in reads:
        copy.start()
    for read, write in zip(reads, writes):
        read.wait()
        write.start()
    for copy in writes:
        copy.wait()


def pack_through(whole):
    rows, width = whole.shape
    out = jax.ShapeDtypeStruct((SIDE, rows, width // SIDE), whole.dtype)
    return pl.pallas_call(
        pack_through_kernel,
        in_specs=[HBM],
        out_specs=HBM,
        out_shape=out,
        scratch_shapes=[pltpu.VMEM(out.shape, out.dtype), pltpu.SemaphoreType.DMA((2, SIDE))],
        compiler_params=room(60),
        cost_estimate=cost(0, out, out),
    )(whole)


def others_kernel(where_ref, all_ref, up_ref, down_ref):
    rows = all_ref.shape[1]
    half = rows // 2
    one, two, three = [lax.rem(where_ref[0] + n, SIDE) for n in (1, 2, 3)]
    up_ref[:rows] = down_ref[rows + half : 2 * rows + half] = all_ref[one]
    up_ref[rows : 2 * rows] = all_ref[two]
    up_ref[2 * rows :] = down_ref[half : rows + half] = all_ref[three]
    down_ref[:half] = all_ref[two, half:]
    down_ref[2 * rows + half :] = all_ref[two, :half]


def others(where, every):
    _, toks, width = every.shape
    out = jax.ShapeDtypeStruct(((SIDE - 1) * toks, width), every.dtype)
    return pl.pallas_call(
        others_kernel,
        in_specs=[SMEM, VMEM],
        out_specs=[VMEM] * 2,
        out_shape=[out] * 2,
        compiler_params=room(8),
        cost_estimate=cost(0, every, every),
    )(where, every)


def halves_swapped(ref):
    half = ref.shape[0] // 2
    return [ref.at[half : 2 * half], ref.at[:half]]


def rows_in_order(where_ref, piece_refs, block, sems):
    each = block.shape[0] // SIDE
    copies = []
    row = 0
    for piece_ref in piece_refs:
        start = row
        while row < start + piece_ref.shape[0]:
            n, skip = divmod(row, each)
            size = min(each - skip, start + piece_ref.shape[0] - row)
            at = pl.multiple_of(lax.rem(where_ref[0] + n, SIDE) * each + skip, each // 2)
            copies.append(
                pltpu.make_async_copy(
                    piece_ref.at[row - start : row - start + size], block.at[pl.ds(at, size)], sems.at[len(copies)]
                )
            )
            row += size
    return copies


def acts_columns(where_ref, shift, acts_ref, depth):
    at = lax.rem(where_ref[1] + shift, SIDE) * depth
    return acts_ref.at[:, pl.ds(pl.multiple_of(at, depth), depth)]


def near_kernel(scale, where_ref, acts_ref, mom_ref, table_ref, *rest):
    pieces, rest = rest[:6], rest[6:]
    part_ref, coeff_ref, high_ref, low_ref, acts_blocks, grad_blocks, mom_block, part_block, sems = rest
    depth = grad_blocks.shape[1]
    own, up, down = pieces[:2], pieces[2:4], pieces[4:]
    down = [*halves_swapped(down[0]), *halves_swapped(down[1])]
    ylo = where_ref[2]
    blocks = []
    for n, (shift, refs) in enumerate(zip((0, 3 - 2 * ylo, 1 + 2 * ylo), (own, up, down))):
        columns = acts_columns(where_ref, shift, acts_ref, depth)
        copies = rows_in_order(where_ref, refs, grad_blocks.at[n], sems.at[n])
        copies.append(pltpu.make_async_copy(columns, acts_blocks.at[n], sems.at[n, 6]))
        blocks.append(copies)
    blocks[2].append(pltpu.make_async_copy(mom_ref, mom_block, sems.at[0, 7]))
    for copies in blocks:
        for copy in copies:
            copy.start()
    rows, coefs = high_ref.shape
    table = jnp.concatenate([table_ref[...]] * (rows // GROUP), 0)
    row = lax.broadcasted_iota(jnp.int32, (rows, coefs), 0) // GROUP
    col = lax.broadcasted_iota(jnp.int32, (rows, coefs), 1) // KEEP
    high, low = two_parts(jnp.where(row == col, table, 0.0))
    high_ref[...], low_ref[...] = high, low
    total = None
    for n, copies in enumerate(blocks):
        for copy in copies:
            copy.wait()
        term = jnp.dot(acts_blocks[n], grad_blocks[n], preferred_element_type=jnp.float32)
        total = term if total is None else total + term
    part = BETA * mom_block[...].astype(jnp.float32) + total * scale
    part_block[...] = part
    out = pltpu.make_async_copy(part_block, part_ref, sems.at[1, 7])
    out.start()
    coeff_ref[...] = dot_parts(two_parts(part), (high, low), ((1,), (0,)))
    out.wait()


def near(scale, where, acts, mom, table, pieces, weight=1):
    feats, toks = acts.shape
    depth = toks // SIDE
    outs = pieces[0].shape[1]
    coefs = table.shape[1]
    part = jax.ShapeDtypeStruct((feats, outs), jnp.float32)
    coeff = jax.ShapeDtypeStruct((feats, coefs), jnp.float32)
    basis = jax.ShapeDtypeStruct((outs, coefs), jnp.bfloat16)
    return pl.pallas_call(
        lambda *refs: near_kernel(scale, *refs),
        in_specs=[SMEM, HBM, HBM, VMEM] + [HBM] * len(pieces),
        out_specs=[HBM] + [VMEM] * 3,
        out_shape=[part, coeff, basis, basis],
        scratch_shapes=[
            pltpu.VMEM((3, feats, depth), jnp.bfloat16),
            pltpu.VMEM((3, depth, outs), jnp.bfloat16),
            pltpu.VMEM(mom.shape, mom.dtype),
            pltpu.VMEM(part.shape, part.dtype),
            pltpu.SemaphoreType.DMA((3, 8)),
        ],
        compiler_params=room(60),
        cost_estimate=cost(weight * 3 * feats * toks * outs // 2, acts, part, *pieces),
    )(where, acts, mom, table, *pieces)


def packed(coeff, rows):
    wide = coeff.shape[1] - LANES
    rest = [coeff[n : n + 8, LANES:] for n in range(0, coeff.shape[0], 8)]
    rest += [jnp.zeros_like(rest[0])] * (-len(rest) % (LANES // wide))
    tiles = [
        jnp.concatenate(rest[n : n + LANES // wide], 1) for n in range(0, len(rest), LANES // wide)
    ]
    blank = jnp.zeros((rows - coeff.shape[0] - 8 * len(tiles), LANES), coeff.dtype)
    return jnp.concatenate([coeff[:, :LANES], *tiles, blank], 0)


def unpacked(tiles, rows, coefs):
    wide = coefs - LANES
    rest = []
    for n in range(rows // 8):
        row, lane = rows + 8 * (n // (LANES // wide)), wide * (n % (LANES // wide))
        rest.append(tiles[row : row + 8, lane : lane + wide])
    return jnp.concatenate([tiles[:rows], jnp.concatenate(rest, 0)], 1)


def far_kernel(
    scale, where_ref, acts_ref, near_ref, high_ref, low_ref, p0_ref, p1_ref, p2_ref, p3_ref,
    packed_ref, acts_block, grad_block, near_block, high_block, low_block, sems,
):
    depth = grad_block.shape[0]
    copies = rows_in_order(where_ref, (p0_ref, p1_ref, p2_ref, p3_ref), grad_block, sems)
    copies.append(pltpu.make_async_copy(high_ref, high_block, sems.at[8]))
    copies.append(pltpu.make_async_copy(low_ref, low_block, sems.at[9]))
    last = [
        pltpu.make_async_copy(
            acts_columns(where_ref, 2, acts_ref, depth), acts_block, sems.at[6]
        ),
        pltpu.make_async_copy(near_ref, near_block, sems.at[7]),
    ]
    for copy in copies + last:
        copy.start()
    for copy in copies:
        copy.wait()

    def dot(a, b):
        return jnp.dot(a, b, preferred_element_type=jnp.float32)

    grad = grad_block[...]
    high, low = two_parts(dot(grad, high_block[...]) + dot(grad, low_block[...]))
    for copy in last:
        copy.wait()
    acts = acts_block[...]
    coeff = near_block[...] + (dot(acts, high) + dot(acts, low)) * scale
    count, rows, _ = packed_ref.shape
    each = coeff.shape[0] // count
    for n in range(count):
        packed_ref[n] = packed(coeff[n * each : (n + 1) * each], rows)


def far(scale, where, acts, coeff, high, low, pieces):
    outs, coefs = high.shape
    feats = acts.shape[0]
    depth = acts.shape[1] // SIDE
    out = jax.ShapeDtypeStruct((16, 64, LANES), jnp.float32)
    return pl.pallas_call(
        lambda *refs: far_kernel(scale, *refs),
        in_specs=[SMEM] + [HBM] * (4 + len(pieces)),
        out_specs=VMEM,
        out_shape=out,
        scratch_shapes=[
            pltpu.VMEM((feats, depth), jnp.bfloat16),
            pltpu.VMEM((depth, outs), jnp.bfloat16),
            pltpu.VMEM(coeff.shape, coeff.dtype),
            pltpu.VMEM(high.shape, high.dtype),
            pltpu.VMEM(low.shape, low.dtype),
            pltpu.SemaphoreType.DMA((10,)),
        ],
        compiler_params=room(58),
        cost_estimate=cost(4 * coefs * depth * (feats + outs), acts, coeff, out, *pieces),
    )(where, acts, coeff, high, low, *pieces)


def residual_kernel(
    scale, where_ref, acts_ref, part_ref, packed_ref, high_ref, low_ref, p0_ref, p1_ref, p2_ref, p3_ref,
    *refs,
):
    outs, (acts_block, grad_block, part_block, sems) = refs[:SIDE], refs[SIDE:]
    x = where_ref[0]
    depth = grad_block.shape[0]
    copies = rows_in_order(where_ref, (p0_ref, p1_ref, p2_ref, p3_ref), grad_block, sems)
    copies.append(
        pltpu.make_async_copy(acts_columns(where_ref, 2, acts_ref, depth), acts_block, sems.at[6])
    )
    copies.append(pltpu.make_async_copy(part_ref, part_block, sems.at[7]))
    for copy in copies:
        copy.start()
    basis = (high_ref[...], low_ref[...])
    count = packed_ref.shape[0]
    each, coefs = part_block.shape[0] // count, high_ref.shape[1]
    coeff = jnp.concatenate([unpacked(packed_ref[n], each, coefs) for n in range(count)], 0)
    kept = dot_parts(two_parts(coeff), basis, ((1,), (1,)))
    for copy in copies:
        copy.wait()
    term = jnp.dot(acts_block[...], grad_block[...], preferred_element_type=jnp.float32)
    part_block[...] = (part_block[...] + term * scale) - kept
    rows = outs[0].shape[0]
    for shift, out_ref in enumerate(outs):
        at = pl.multiple_of(lax.rem(x + shift, SIDE) * rows, rows)
        out_ref[...] = part_block[pl.ds(at, rows), :].astype(jnp.bfloat16)


def residual(scale, where, acts, part, coeff, high, low, pieces):
    feats, outs = part.shape
    depth = acts.shape[1] // SIDE
    fresh = jax.ShapeDtypeStruct((feats // SIDE, outs), jnp.bfloat16)
    return pl.pallas_call(
        lambda *refs: residual_kernel(scale, *refs),
        in_specs=[SMEM] + [HBM] * 2 + [VMEM] * 3 + [HBM] * len(pieces),
        out_specs=[VMEM] * SIDE,
        out_shape=[fresh] * SIDE,
        scratch_shapes=[
            pltpu.VMEM((feats, depth), jnp.bfloat16),
            pltpu.VMEM((depth, outs), jnp.bfloat16),
            pltpu.VMEM(part.shape, part.dtype),
            pltpu.SemaphoreType.DMA((8,)),
        ],
        compiler_params=room(60),
        cost_estimate=cost(feats * outs * (2 * depth + 960), part, coeff, *[fresh] * SIDE),
    )(where, acts, part, coeff, high, low, *pieces)


def decode_kernel(replicas, total_ref, high_ref, low_ref, update_ref):
    rows = update_ref.shape[0]
    width, coefs = high_ref.shape
    basis = (high_ref[...], low_ref[...])
    for q in range(SIDE):
        quarters = []
        for ylo in range(2):
            for core in range(2):
                tiles = jnp.concatenate([total_ref[core, ylo, q, 0], total_ref[core, ylo, q, 1]], 0)
                quarters.append(unpacked(tiles, rows // 4, coefs))
        mean = two_parts(jnp.concatenate(quarters, 0) / replicas)
        update_ref[:, q * width : (q + 1) * width] = dot_parts(mean, basis, ((1,), (1,))).astype(
            jnp.bfloat16
        )


def decode(replicas, rows, total, high, low):
    out = jax.ShapeDtypeStruct((rows, SIDE * high.shape[0]), jnp.bfloat16)
    return pl.pallas_call(
        lambda *refs: decode_kernel(replicas, *refs),
        in_specs=[VMEM] * 3,
        out_specs=VMEM,
        out_shape=out,
        compiler_params=room(8),
        cost_estimate=cost(6 * total.size * high.shape[0], total, out),
    )(total, high, low)


def columns_kernel(where_ref, *refs):
    *pieces, out_ref = refs
    width = pieces[0].shape[1]
    for n, piece_ref in enumerate(pieces):
        at = lax.rem(where_ref[0] + SIDE - n, SIDE) * width
        out_ref[:, pl.ds(pl.multiple_of(at, width), width)] = piece_ref[...]


def columns(where, pieces):
    rows, width = pieces[0].shape
    out = jax.ShapeDtypeStruct((rows, SIDE * width), pieces[0].dtype)
    return pl.pallas_call(
        columns_kernel,
        in_specs=[SMEM] + [VMEM] * SIDE,
        out_specs=VMEM,
        out_shape=out,
        compiler_params=room(4),
        cost_estimate=cost(0, out, out),
    )(where, *pieces)


def y_shifted(x, by):
    pairs = []
    for ylo, step in ((0, by), (1, -by)):
        pairs += [(SIDE * ylo + i, SIDE * ylo + (i + step) % SIDE) for i in range(SIDE)]
    return lax.ppermute(x, ("ylo", "yhi"), pairs)


def shifted(x, axis, by):
    return lax.ppermute(x, axis, [(i, (i + by) % SIDE) for i in range(SIDE)])


def per_device(attn_out, out_grad, momentum, kept):
    replicas = 32
    scale = 1.0 / math.sqrt(attn_out.shape[0])
    toks, width = out_grad.shape
    where = jnp.stack([lax.axis_index(name) for name in ("x", "yhi", "ylo")]).astype(jnp.int32)

    acts = lax.all_gather(attn_out.T, "x", axis=0, tiled=True)
    first, swapped = quarter(where, out_grad)
    up, down = [y_shifted(first, 1)], [y_shifted(swapped, -1)]
    every = lax.all_to_all(pack_through(out_grad), "x", 0, 0, tiled=True)
    every, up[0], down[0] = lax.optimization_barrier((every, up[0], down[0]))
    rest, swapped = others(where, every)
    stored, rest, swapped = lax.optimization_barrier((momentum[0], rest, swapped))
    mom = lax.all_to_all(pack(stored, 60), "x", 0, 0, tiled=True).reshape(SIDE * toks, width // SIDE)
    own = [first, rest]
    up.append(y_shifted(rest, 1))
    down.append(y_shifted(swapped, -1))
    over = []
    for above, below in zip(up, down):
        middle = above.shape[0] // 2
        over.append(y_shifted(above[:middle], 1))
        over.append(y_shifted(below[:middle], -1))

    table = basis_table(jnp.tile(kept, width // SIDE // GROUP))
    part, coeff, high, low = near(scale, where, acts, mom, table, own + up + down, 20)
    pieces = far(scale, where, acts, coeff, high, low, over)
    fresh = residual(scale, where, acts, part, pieces, high, low, over)

    tile = pieces.shape[1:]
    pieces = lax.all_to_all(pieces, ("x", "ylo", "core"), 0, 0, tiled=True)
    summed = pieces.reshape(4, 4, *tile).sum(1)
    tile = (tile[0] // 2, tile[1])
    summed, *fresh = lax.optimization_barrier((summed, *fresh))
    pieces = lax.all_to_all(summed.reshape(8, *tile), "z", 0, 0, tiled=True)
    summed = pieces.sum(0)
    spread = jnp.broadcast_to(summed[None], (16, *tile))
    spread = lax.all_to_all(spread, ("ylo", "z"), 0, 0, tiled=True)
    total = lax.all_gather(spread, "core", axis=0).reshape(2, 2, 4, 2, *tile)
    fresh = [fresh[0]] + [shifted(fresh[s], "x", s) for s in (1, 2, 3)]
    update = decode(replicas, toks, total, high, low)
    total, *fresh = lax.optimization_barrier((total, *fresh))
    new_momentum = columns(where, fresh)
    return update, new_momentum[None]


def solution(mesh):
    fine = Mesh(mesh.devices.reshape(2, 8, 2, 4, 4), ("ylo", "z", "core", "yhi", "x"))
    return jax.shard_map(
        per_device,
        mesh=fine,
        in_specs=(P(REP, FSDP), P(REP + FSDP, None), P(REP, FSDP, None), P()),
        out_specs=(P(FSDP, None), P(REP, FSDP, None)),
        check_vma=False,
    )
```

```python
import math

import jax
import jax.numpy as jnp
from jax import lax
from jax.experimental import pallas as pl
from jax.experimental.pallas import tpu as pltpu
from jax.sharding import Mesh, PartitionSpec as P

GROUP = 64
KEEP = 16
BETA = 0.999
SIDE = 4
LANES = 128

REP = ("ylo", "z", "core")
FSDP = ("yhi", "x")

SMEM = pl.BlockSpec(memory_space=pltpu.SMEM)
VMEM = pl.BlockSpec(memory_space=pltpu.VMEM)
HBM = pl.BlockSpec(memory_space=pltpu.HBM)


def room(mebibytes):
    return pltpu.CompilerParams(vmem_limit_bytes=mebibytes * 1024 * 1024)


def basis_table(kept):
    freq = kept.astype(jnp.float32)
    points = jnp.arange(GROUP, dtype=jnp.float32) + 0.5
    weight = jnp.where(kept == 0, math.sqrt(1.0 / GROUP), math.sqrt(2.0 / GROUP)).astype(
        jnp.float32
    )
    return weight[None, :] * jnp.cos(math.pi * points[:, None] * freq[None, :] / GROUP)


def cost(flops, *arrays):
    return pl.CostEstimate(
        flops=flops, bytes_accessed=sum(a.size * a.dtype.itemsize for a in arrays), transcendentals=0
    )


def two_parts(x):
    high = x.astype(jnp.bfloat16)
    return high, (x - high.astype(jnp.float32)).astype(jnp.bfloat16)


def dot_parts(a, b, dims):
    def one(x, y):
        return lax.dot_general(x, y, (dims, ((), ())), preferred_element_type=jnp.float32)

    return one(a[0], b[0]) + (one(a[0], b[1]) + one(a[1], b[0]))


def quarter_kernel(where_ref, grad_ref, up_ref, down_ref):
    rows, width = up_ref.shape
    half = rows // 2
    at = pl.multiple_of(where_ref[0] * width, width)
    up_ref[...] = grad_ref[:, pl.ds(at, width)]
    down_ref[:half] = grad_ref[half:, pl.ds(at, width)]
    down_ref[half:] = grad_ref[:half, pl.ds(at, width)]


def quarter(where, whole):
    rows, width = whole.shape
    out = jax.ShapeDtypeStruct((rows, width // SIDE), whole.dtype)
    return pl.pallas_call(
        quarter_kernel,
        in_specs=[SMEM, VMEM],
        out_specs=[VMEM] * 2,
        out_shape=[out] * 2,
        compiler_params=room(4),
        cost_estimate=cost(0, out, out),
    )(where, whole)


def pack_kernel(whole_ref, out_ref):
    width = out_ref.shape[2]
    for q in range(SIDE):
        out_ref[q] = whole_ref[:, q * width : (q + 1) * width]


def pack(whole, weight=1):
    rows, width = whole.shape
    out = jax.ShapeDtypeStruct((SIDE, rows, width // SIDE), whole.dtype)
    return pl.pallas_call(
        pack_kernel,
        in_specs=[VMEM],
        out_specs=VMEM,
        out_shape=out,
        compiler_params=room(4),
        cost_estimate=cost(0, *[out] * weight),
    )(whole)


def pack_through_kernel(whole_ref, out_ref, block, sems):
    width = out_ref.shape[2]
    reads, writes = [], []
    for q in range(SIDE):
        span = slice(q * width, (q + 1) * width)
        reads.append(pltpu.make_async_copy(whole_ref.at[:, span], block.at[q], sems.at[0, q]))
        writes.append(pltpu.make_async_copy(block.at[q], out_ref.at[q], sems.at[1, q]))
    for copy in reads:
        copy.start()
    for read, write in zip(reads, writes):
        read.wait()
        write.start()
    for copy in writes:
        copy.wait()


def pack_through(whole):
    rows, width = whole.shape
    out = jax.ShapeDtypeStruct((SIDE, rows, width // SIDE), whole.dtype)
    return pl.pallas_call(
        pack_through_kernel,
        in_specs=[HBM],
        out_specs=HBM,
        out_shape=out,
        scratch_shapes=[pltpu.VMEM(out.shape, out.dtype), pltpu.SemaphoreType.DMA((2, SIDE))],
        compiler_params=room(60),
        cost_estimate=cost(0, out, out),
    )(whole)


def others_kernel(where_ref, all_ref, up_ref, down_ref):
    rows = all_ref.shape[1]
    half = rows // 2
    one, two, three = [lax.rem(where_ref[0] + n, SIDE) for n in (1, 2, 3)]
    up_ref[:rows] = down_ref[rows + half : 2 * rows + half] = all_ref[one]
    up_ref[rows : 2 * rows] = all_ref[two]
    up_ref[2 * rows :] = down_ref[half : rows + half] = all_ref[three]
    down_ref[:half] = all_ref[two, half:]
    down_ref[2 * rows + half :] = all_ref[two, :half]


def others(where, every):
    _, toks, width = every.shape
    out = jax.ShapeDtypeStruct(((SIDE - 1) * toks, width), every.dtype)
    return pl.pallas_call(
        others_kernel,
        in_specs=[SMEM, VMEM],
        out_specs=[VMEM] * 2,
        out_shape=[out] * 2,
        compiler_params=room(8),
        cost_estimate=cost(0, every, every),
    )(where, every)


def halves_swapped(ref):
    half = ref.shape[0] // 2
    return [ref.at[half : 2 * half], ref.at[:half]]


def rows_in_order(where_ref, piece_refs, block, sems):
    each = block.shape[0] // SIDE
    copies = []
    row = 0
    for piece_ref in piece_refs:
        start = row
        while row < start + piece_ref.shape[0]:
            n, skip = divmod(row, each)
            size = min(each - skip, start + piece_ref.shape[0] - row)
            at = pl.multiple_of(lax.rem(where_ref[0] + n, SIDE) * each + skip, each // 2)
            copies.append(
                pltpu.make_async_copy(
                    piece_ref.at[row - start : row - start + size], block.at[pl.ds(at, size)], sems.at[len(copies)]
                )
            )
            row += size
    return copies


def acts_columns(where_ref, shift, acts_ref, depth):
    at = lax.rem(where_ref[1] + shift, SIDE) * depth
    return acts_ref.at[:, pl.ds(pl.multiple_of(at, depth), depth)]


def near_kernel(scale, where_ref, acts_ref, mom_ref, table_ref, *rest):
    pieces, rest = rest[:6], rest[6:]
    part_ref, coeff_ref, high_ref, low_ref, acts_blocks, grad_blocks, mom_block, part_block, sems = rest
    depth = grad_blocks.shape[1]
    own, up, down = pieces[:2], pieces[2:4], pieces[4:]
    down = [*halves_swapped(down[0]), *halves_swapped(down[1])]
    ylo = where_ref[2]
    blocks = []
    for n, (shift, refs) in enumerate(zip((0, 3 - 2 * ylo, 1 + 2 * ylo), (own, up, down))):
        columns = acts_columns(where_ref, shift, acts_ref, depth)
        copies = rows_in_order(where_ref, refs, grad_blocks.at[n], sems.at[n])
        copies.append(pltpu.make_async_copy(columns, acts_blocks.at[n], sems.at[n, 6]))
        blocks.append(copies)
    blocks[2].append(pltpu.make_async_copy(mom_ref, mom_block, sems.at[0, 7]))
    for copies in blocks:
        for copy in copies:
            copy.start()
    rows, coefs = high_ref.shape
    table = jnp.concatenate([table_ref[...]] * (rows // GROUP), 0)
    row = lax.broadcasted_iota(jnp.int32, (rows, coefs), 0) // GROUP
    col = lax.broadcasted_iota(jnp.int32, (rows, coefs), 1) // KEEP
    high, low = two_parts(jnp.where(row == col, table, 0.0))
    high_ref[...], low_ref[...] = high, low
    total = None
    for n, copies in enumerate(blocks):
        for copy in copies:
            copy.wait()
        term = jnp.dot(acts_blocks[n], grad_blocks[n], preferred_element_type=jnp.float32)
        total = term if total is None else total + term
    part = BETA * mom_block[...].astype(jnp.float32) + total * scale
    part_block[...] = part
    out = pltpu.make_async_copy(part_block, part_ref, sems.at[1, 7])
    out.start()
    coeff_ref[...] = dot_parts(two_parts(part), (high, low), ((1,), (0,)))
    out.wait()


def near(scale, where, acts, mom, table, pieces, weight=1):
    feats, toks = acts.shape
    depth = toks // SIDE
    outs = pieces[0].shape[1]
    coefs = table.shape[1]
    part = jax.ShapeDtypeStruct((feats, outs), jnp.float32)
    coeff = jax.ShapeDtypeStruct((feats, coefs), jnp.float32)
    basis = jax.ShapeDtypeStruct((outs, coefs), jnp.bfloat16)
    return pl.pallas_call(
        lambda *refs: near_kernel(scale, *refs),
        in_specs=[SMEM, HBM, HBM, VMEM] + [HBM] * len(pieces),
        out_specs=[HBM] + [VMEM] * 3,
        out_shape=[part, coeff, basis, basis],
        scratch_shapes=[
            pltpu.VMEM((3, feats, depth), jnp.bfloat16),
            pltpu.VMEM((3, depth, outs), jnp.bfloat16),
            pltpu.VMEM(mom.shape, mom.dtype),
            pltpu.VMEM(part.shape, part.dtype),
            pltpu.SemaphoreType.DMA((3, 8)),
        ],
        compiler_params=room(60),
        cost_estimate=cost(weight * 3 * feats * toks * outs // 2, acts, part, *pieces),
    )(where, acts, mom, table, *pieces)


def packed(coeff, rows):
    wide = coeff.shape[1] - LANES
    rest = [coeff[n : n + 8, LANES:] for n in range(0, coeff.shape[0], 8)]
    rest += [jnp.zeros_like(rest[0])] * (-len(rest) % (LANES // wide))
    tiles = [
        jnp.concatenate(rest[n : n + LANES // wide], 1) for n in range(0, len(rest), LANES // wide)
    ]
    blank = jnp.zeros((rows - coeff.shape[0] - 8 * len(tiles), LANES), coeff.dtype)
    return jnp.concatenate([coeff[:, :LANES], *tiles, blank], 0)


def unpacked(tiles, rows, coefs):
    wide = coefs - LANES
    rest = []
    for n in range(rows // 8):
        row, lane = rows + 8 * (n // (LANES // wide)), wide * (n % (LANES // wide))
        rest.append(tiles[row : row + 8, lane : lane + wide])
    return jnp.concatenate([tiles[:rows], jnp.concatenate(rest, 0)], 1)


def far_kernel(
    scale, where_ref, acts_ref, near_ref, high_ref, low_ref, p0_ref, p1_ref, p2_ref, p3_ref,
    packed_ref, acts_block, grad_block, near_block, high_block, low_block, sems,
):
    depth = grad_block.shape[0]
    copies = rows_in_order(where_ref, (p0_ref, p1_ref, p2_ref, p3_ref), grad_block, sems)
    copies.append(pltpu.make_async_copy(high_ref, high_block, sems.at[8]))
    copies.append(pltpu.make_async_copy(low_ref, low_block, sems.at[9]))
    last = [
        pltpu.make_async_copy(
            acts_columns(where_ref, 2, acts_ref, depth), acts_block, sems.at[6]
        ),
        pltpu.make_async_copy(near_ref, near_block, sems.at[7]),
    ]
    for copy in copies + last:
        copy.start()
    for copy in copies:
        copy.wait()

    def dot(a, b):
        return jnp.dot(a, b, preferred_element_type=jnp.float32)

    grad = grad_block[...]
    encoded = []
    for start in range(0, depth, 256):
        stop = min(start + 256, depth)
        span = slice(start // GROUP * KEEP, stop // GROUP * KEEP)
        both = jnp.concatenate([high_block[start:stop, span], low_block[start:stop, span]], 1)
        parts = dot(grad[:, start:stop], both)
        wide = span.stop - span.start
        encoded.append(parts[:, :wide] + parts[:, wide:])
    high, low = two_parts(jnp.concatenate(encoded, 1))
    for copy in last:
        copy.wait()
    acts = acts_block[...]
    coeff = near_block[...] + (dot(acts, high) + dot(acts, low)) * scale
    count, rows, _ = packed_ref.shape
    each = coeff.shape[0] // count
    for n in range(count):
        packed_ref[n] = packed(coeff[n * each : (n + 1) * each], rows)


def far(scale, where, acts, coeff, high, low, pieces):
    outs, coefs = high.shape
    feats = acts.shape[0]
    depth = acts.shape[1] // SIDE
    out = jax.ShapeDtypeStruct((16, 64, LANES), jnp.float32)
    return pl.pallas_call(
        lambda *refs: far_kernel(scale, *refs),
        in_specs=[SMEM] + [HBM] * (4 + len(pieces)),
        out_specs=VMEM,
        out_shape=out,
        scratch_shapes=[
            pltpu.VMEM((feats, depth), jnp.bfloat16),
            pltpu.VMEM((depth, outs), jnp.bfloat16),
            pltpu.VMEM(coeff.shape, coeff.dtype),
            pltpu.VMEM(high.shape, high.dtype),
            pltpu.VMEM(low.shape, low.dtype),
            pltpu.SemaphoreType.DMA((10,)),
        ],
        compiler_params=room(58),
        cost_estimate=cost(4 * coefs * depth * (feats + outs), acts, coeff, out, *pieces),
    )(where, acts, coeff, high, low, *pieces)


def residual_kernel(
    scale, where_ref, acts_ref, part_ref, packed_ref, high_ref, low_ref, p0_ref, p1_ref, p2_ref, p3_ref,
    *refs,
):
    outs, (acts_block, grad_block, part_block, sems) = refs[:SIDE], refs[SIDE:]
    x = where_ref[0]
    depth = grad_block.shape[0]
    copies = rows_in_order(where_ref, (p0_ref, p1_ref, p2_ref, p3_ref), grad_block, sems)
    copies.append(
        pltpu.make_async_copy(acts_columns(where_ref, 2, acts_ref, depth), acts_block, sems.at[6])
    )
    copies.append(pltpu.make_async_copy(part_ref, part_block, sems.at[7]))
    for copy in copies:
        copy.start()
    basis = (high_ref[...], low_ref[...])
    count = packed_ref.shape[0]
    each, coefs = part_block.shape[0] // count, high_ref.shape[1]
    coeff = jnp.concatenate([unpacked(packed_ref[n], each, coefs) for n in range(count)], 0)
    kept = dot_parts(two_parts(coeff), basis, ((1,), (1,)))
    for copy in copies:
        copy.wait()
    term = jnp.dot(acts_block[...], grad_block[...], preferred_element_type=jnp.float32)
    part_block[...] = (part_block[...] + term * scale) - kept
    rows = outs[0].shape[0]
    for shift, out_ref in enumerate(outs):
        at = pl.multiple_of(lax.rem(x + shift, SIDE) * rows, rows)
        out_ref[...] = part_block[pl.ds(at, rows), :].astype(jnp.bfloat16)


def residual(scale, where, acts, part, coeff, high, low, pieces):
    feats, outs = part.shape
    depth = acts.shape[1] // SIDE
    fresh = jax.ShapeDtypeStruct((feats // SIDE, outs), jnp.bfloat16)
    return pl.pallas_call(
        lambda *refs: residual_kernel(scale, *refs),
        in_specs=[SMEM] + [HBM] * 2 + [VMEM] * 3 + [HBM] * len(pieces),
        out_specs=[VMEM] * SIDE,
        out_shape=[fresh] * SIDE,
        scratch_shapes=[
            pltpu.VMEM((feats, depth), jnp.bfloat16),
            pltpu.VMEM((depth, outs), jnp.bfloat16),
            pltpu.VMEM(part.shape, part.dtype),
            pltpu.SemaphoreType.DMA((8,)),
        ],
        compiler_params=room(60),
        cost_estimate=cost(feats * outs * (2 * depth + 960), part, coeff, *[fresh] * SIDE),
    )(where, acts, part, coeff, high, low, *pieces)


def decode_kernel(replicas, total_ref, high_ref, low_ref, update_ref):
    rows = update_ref.shape[0]
    width, coefs = high_ref.shape
    basis = (high_ref[...], low_ref[...])
    for q in range(SIDE):
        quarters = []
        for ylo in range(2):
            for core in range(2):
                tiles = jnp.concatenate([total_ref[core, ylo, q, 0], total_ref[core, ylo, q, 1]], 0)
                quarters.append(unpacked(tiles, rows // 4, coefs))
        mean = two_parts(jnp.concatenate(quarters, 0) / replicas)
        update_ref[:, q * width : (q + 1) * width] = dot_parts(mean, basis, ((1,), (1,))).astype(
            jnp.bfloat16
        )


def decode(replicas, rows, total, high, low):
    out = jax.ShapeDtypeStruct((rows, SIDE * high.shape[0]), jnp.bfloat16)
    return pl.pallas_call(
        lambda *refs: decode_kernel(replicas, *refs),
        in_specs=[VMEM] * 3,
        out_specs=VMEM,
        out_shape=out,
        compiler_params=room(8),
        cost_estimate=cost(6 * total.size * high.shape[0], total, out),
    )(total, high, low)


def columns_kernel(where_ref, *refs):
    *pieces, out_ref = refs
    width = pieces[0].shape[1]
    for n, piece_ref in enumerate(pieces):
        at = lax.rem(where_ref[0] + SIDE - n, SIDE) * width
        out_ref[:, pl.ds(pl.multiple_of(at, width), width)] = piece_ref[...]


def columns(where, pieces):
    rows, width = pieces[0].shape
    out = jax.ShapeDtypeStruct((rows, SIDE * width), pieces[0].dtype)
    return pl.pallas_call(
        columns_kernel,
        in_specs=[SMEM] + [VMEM] * SIDE,
        out_specs=VMEM,
        out_shape=out,
        compiler_params=room(4),
        cost_estimate=cost(0, out, out),
    )(where, *pieces)


def y_shifted(x, by):
    pairs = []
    for ylo, step in ((0, by), (1, -by)):
        pairs += [(SIDE * ylo + i, SIDE * ylo + (i + step) % SIDE) for i in range(SIDE)]
    return lax.ppermute(x, ("ylo", "yhi"), pairs)


def shifted(x, axis, by):
    return lax.ppermute(x, axis, [(i, (i + by) % SIDE) for i in range(SIDE)])


def per_device(attn_out, out_grad, momentum, kept):
    replicas = 32
    scale = 1.0 / math.sqrt(attn_out.shape[0])
    toks, width = out_grad.shape
    where = jnp.stack([lax.axis_index(name) for name in ("x", "yhi", "ylo")]).astype(jnp.int32)

    acts = lax.all_gather(attn_out.T, "x", axis=0, tiled=True)
    first, swapped = quarter(where, out_grad)
    up, down = [y_shifted(first, 1)], [y_shifted(swapped, -1)]
    every = lax.all_to_all(pack_through(out_grad), "x", 0, 0, tiled=True)
    every, up[0], down[0] = lax.optimization_barrier((every, up[0], down[0]))
    rest, swapped = others(where, every)
    stored, rest, swapped = lax.optimization_barrier((momentum[0], rest, swapped))
    mom = lax.all_to_all(pack(stored, 60), "x", 0, 0, tiled=True).reshape(SIDE * toks, width // SIDE)
    own = [first, rest]
    up.append(y_shifted(rest, 1))
    down.append(y_shifted(swapped, -1))
    over = []
    for above, below in zip(up, down):
        middle = above.shape[0] // 2
        over.append(y_shifted(above[:middle], 1))
        over.append(y_shifted(below[:middle], -1))

    table = basis_table(jnp.tile(kept, width // SIDE // GROUP))
    part, coeff, high, low = near(scale, where, acts, mom, table, own + up + down, 20)
    pieces = far(scale, where, acts, coeff, high, low, over)
    fresh = residual(scale, where, acts, part, pieces, high, low, over)

    tile = pieces.shape[1:]
    pieces = lax.all_to_all(pieces, ("x", "ylo", "core"), 0, 0, tiled=True)
    summed = pieces.reshape(4, 4, *tile).sum(1)
    tile = (tile[0] // 2, tile[1])
    summed, *fresh = lax.optimization_barrier((summed, *fresh))
    pieces = lax.all_to_all(summed.reshape(8, *tile), "z", 0, 0, tiled=True)
    summed = pieces.sum(0)
    spread = jnp.broadcast_to(summed[None], (16, *tile))
    spread = lax.all_to_all(spread, ("ylo", "z"), 0, 0, tiled=True)
    total = lax.all_gather(spread, "core", axis=0).reshape(2, 2, 4, 2, *tile)
    fresh = [fresh[0]] + [shifted(fresh[s], "x", s) for s in (1, 2, 3)]
    update = decode(replicas, toks, total, high, low)
    total, *fresh = lax.optimization_barrier((total, *fresh))
    new_momentum = columns(where, fresh)
    return update, new_momentum[None]


def solution(mesh):
    fine = Mesh(mesh.devices.reshape(2, 8, 2, 4, 4), ("ylo", "z", "core", "yhi", "x"))
    return jax.shard_map(
        per_device,
        mesh=fine,
        in_specs=(P(REP, FSDP), P(REP + FSDP, None), P(REP, FSDP, None), P()),
        out_specs=(P(FSDP, None), P(REP, FSDP, None)),
        check_vma=False,
    )
```
